256 devices in a mesh: dp: 4 (over x), seq: 32 (over y_hi, z, core), aud: 2 (over y_lo).
Axes of the slice: x: 4, y: 4 (y_hi: 2, y_lo: 2; y = y_hi * 2 + y_lo), z: 8, core: 2. Of those that a mesh axis runs over, the one named last changes fastest.
Arguments:
- q_video: bfloat16 [32768, 3072], P(('dp', 'seq', 'aud')), parts along dimension 0, may hold values from -8 to 8
- k_video: bfloat16 [32768, 3072], P(('dp', 'seq', 'aud')), parts along dimension 0, may hold values from -8 to 8
- v_video: bfloat16 [32768, 3072], P(('dp', 'seq', 'aud')), parts along dimension 0, may hold values from -6 to 6
- d_video: bfloat16 [32768, 3072], P(('dp', 'seq', 'aud')), parts along dimension 0, may hold values from -6 to 6
- q_audio: bfloat16 [1024, 3072], P(('dp', 'seq', 'aud')), parts along dimension 0, may hold values from -8 to 8
- k_audio: bfloat16 [1024, 3072], P(('dp', 'seq', 'aud')), parts along dimension 0, may hold values from -8 to 8
- v_audio: bfloat16 [1024, 3072], P(('dp', 'seq', 'aud')), parts along dimension 0, may hold values from -6 to 6
- d_audio: bfloat16 [1024, 3072], P(('dp', 'seq', 'aud')), parts along dimension 0, may hold values from -6 to 6
- audio_pos: int32 [1024], P(('dp', 'seq', 'aud')), parts along dimension 0, may hold values from 0 to 15
- video_len: int32 [4], P('dp'), parts along dimension 0, may hold values from 4096 to 8192
- audio_len: int32 [4], P('dp'), parts along dimension 0, may hold values from 128 to 256
Outputs:
- dk_video: bfloat16 [32768, 3072], P(('dp', 'seq', 'aud')), parts along dimension 0
- dv_video: bfloat16 [32768, 3072], P(('dp', 'seq', 'aud')), parts along dimension 0
- dk_audio: bfloat16 [1024, 3072], P(('dp', 'seq', 'aud')), parts along dimension 0
- dv_audio: bfloat16 [1024, 3072], P(('dp', 'seq', 'aud')), parts along dimension 0
The draws below stay inside these ranges and needn't reach their ends.
There are 4 independent parts, one for each index of `dp`. The reference program is written for one: setup_inputs(seed, part) draws one part's arguments, and reference() takes and returns one part's arrays. A program takes and returns all parts, laid end to end along the dimension named above; each array names one. Nothing has to cross between parts.
All inputs are finite; a program needn't handle non-finite values.
Results may differ from the reference program's by a relative error of at most 0.011.
Values may be sent and summed in bfloat16 or wider, within the bound.
No kernel may reach another device: no remote copies, remote signals or barrier semaphores. Data moves between devices by JAX's collectives and lax.ppermute only.
A program may use at most 128 MiB of HBM per device.

```python
import jax
import jax.numpy as jnp
from jax import lax

D = 3072
HD = 128
VFRAME = 512
VTOK_DEV = 128
VIDEO = 8192
AUDIO = 256


def drawn_rows(key, row_count):
    return jnp.clip(jax.random.normal(key, (row_count, D), jnp.float32), -4.0, 4.0)


def draw_q_video(key, part):
    key = jax.random.fold_in(key, 1)
    values = drawn_rows(key, VIDEO)
    return values.astype(jnp.bfloat16)


def draw_k_audio(key, part):
    key = jax.random.fold_in(key, 2)
    values = drawn_rows(key, AUDIO)
    return values.astype(jnp.bfloat16)


def draw_q_audio(key, part):
    key = jax.random.fold_in(key, 3)
    values = drawn_rows(key, AUDIO)
    return values.astype(jnp.bfloat16)


def draw_k_video(key, part):
    key = jax.random.fold_in(key, 4)
    values = drawn_rows(key, VIDEO)
    return values.astype(jnp.bfloat16)


def plant(drawn, rng, smallest, largest):
    shape = drawn.shape
    index_at = [jax.random.randint(jax.random.fold_in(rng, axis), (), 0, shape[axis]) for axis in range(len(shape))]
    drawn = drawn.at[tuple(index_at)].set(smallest)
    longest = shape.index(max(shape))
    index_at[longest] = (index_at[longest] + 1) % shape[longest]
    return drawn.at[tuple(index_at)].set(largest)


def block_scale(stream_key, shape, shards, smallest, high):
    gain = 1.0
    for dim, shards_of in shards:
        draws = jax.random.uniform(jax.random.fold_in(jax.random.fold_in(stream_key, 6), dim), (shards_of,), jnp.float32, smallest / len(shards), high / len(shards))
        gain = gain * jnp.repeat(jnp.exp(draws), shape[dim] // shards_of).reshape((-1,) + (1,) * (len(shape) - 1 - dim))
    return gain


def centred(stream_key, dims, scale, limit, cuts=(), kind=jnp.bfloat16):
    gain = block_scale(stream_key, dims, cuts, -0.22, 0.18) if cuts else 1.0
    entries = jax.random.normal(stream_key, dims, jnp.float32) * scale * gain
    return jnp.minimum(jnp.maximum(entries, -limit), limit).astype(kind)


def setup_inputs(seed: int = 0, part: int = 0) -> dict:
    splits = jax.random.split(jax.random.key(seed), 12)
    part_keys = jax.random.split(jax.random.fold_in(splits[11], part), 12)
    q_video = draw_q_video(jax.random.fold_in(jax.random.fold_in(splits[11], part), 71), part)
    k_video = draw_k_video(jax.random.fold_in(jax.random.fold_in(splits[11], part), 71), part)
    v_video = centred(part_keys[2], (VIDEO, D), 1.0, 6.0, ((0, 64),))
    d_video = centred(part_keys[3], (VIDEO, D), 1.0, 6.0, ((0, 64),))
    q_audio = draw_q_audio(jax.random.fold_in(jax.random.fold_in(splits[11], part), 71), part)
    k_audio = draw_k_audio(jax.random.fold_in(jax.random.fold_in(splits[11], part), 71), part)
    v_audio = centred(part_keys[6], (AUDIO, D), 1.0, 6.0, ((0, 64),))
    d_audio = centred(part_keys[7], (AUDIO, D), 1.0, 6.0, ((0, 64),))
    audio_pos = plant(jax.random.randint(part_keys[8], (AUDIO,), 0, VIDEO // VFRAME), jax.random.fold_in(part_keys[8], 1), 0, (VIDEO // VFRAME) - 1).astype(jnp.int32)
    video_len = jax.random.randint(part_keys[9], (1,), VIDEO // 2, VIDEO + 1).astype(jnp.int32)
    audio_len = jax.random.randint(part_keys[10], (1,), AUDIO // 2, AUDIO + 1).astype(jnp.int32)
    return {"q_video": q_video, "k_video": k_video, "v_video": v_video, "d_video": d_video, "q_audio": q_audio, "k_audio": k_audio, "v_audio": v_audio, "d_audio": d_audio, "audio_pos": audio_pos, "video_len": video_len, "audio_len": audio_len}


rope_base = 10000.0
neg_fill = -1.0e30


def rotate(values, where_at, direction):
    row_count = values.shape[0]
    half_width = HD // 2
    frequency = rope_base ** (-(jnp.arange(half_width, dtype=jnp.float32) / half_width))
    phase_angle = where_at.astype(jnp.float32)[:, None] * frequency[None, :]
    cosine = jnp.cos(phase_angle)[:, None, :]
    sine_part = direction * jnp.sin(phase_angle)[:, None, :]
    shaped = values.astype(jnp.float32).reshape(row_count, -1, HD)
    first_half = shaped[:, :, :half_width]
    second = shaped[:, :, half_width:]
    turned = jnp.concatenate([first_half * cosine - second * sine_part, second * cosine + first_half * sine_part], axis=2)
    return turned.reshape(row_count, -1)


def split_heads(values):
    return values.astype(jnp.float32).reshape(values.shape[0], -1, HD)


def rounded(values):
    return lax.optimization_barrier(values.astype(jnp.bfloat16)).astype(jnp.float32)


def reference(q_video, k_video, v_video, d_video, q_audio, k_audio, v_audio, d_audio, audio_pos, video_len, audio_len):
    score_scale = HD ** -0.5
    video_pos = jnp.arange(VIDEO, dtype=jnp.int32) // VFRAME
    video_query = rotate(q_video, video_pos, 1.0).astype(jnp.bfloat16)
    video_key = rotate(k_video, video_pos, 1.0).astype(jnp.bfloat16)
    audio_query = rotate(q_audio, audio_pos, 1.0).astype(jnp.bfloat16)
    audio_key = rotate(k_audio, audio_pos, 1.0).astype(jnp.bfloat16)
    video_valid = jnp.arange(VIDEO, dtype=jnp.int32) < video_len[0]
    audio_valid = jnp.arange(AUDIO, dtype=jnp.int32) < audio_len[0]
    video_grad = jnp.where(video_valid[:, None], d_video, jnp.zeros_like(d_video))
    audio_grad = jnp.where(audio_valid[:, None], d_audio, jnp.zeros_like(d_audio))
    blocks = VIDEO // VTOK_DEV
    key_heads = split_heads(audio_key)
    value_heads = split_heads(v_audio)

    def video_step(carry, pieces):
        query_block, grad_block = pieces
        query_heads = split_heads(query_block)
        grad_heads = split_heads(grad_block)
        scores = jnp.einsum("qhd,khd->qhk", query_heads, key_heads) * score_scale
        scores = jnp.where(audio_valid[None, None, :], scores, neg_fill)
        raw_weights = jnp.exp(scores - jnp.max(scores, axis=2, keepdims=True))
        probs = raw_weights / jnp.sum(raw_weights, axis=2, keepdims=True)
        probs_low = rounded(probs)
        outputs = jnp.einsum("qhk,khd->qhd", probs_low, value_heads)
        delta = jnp.sum(grad_heads * outputs, axis=2)
        dprobs = jnp.einsum("qhd,khd->qhk", grad_heads, value_heads)
        dscores = rounded(probs * (dprobs - delta[:, :, None]) * score_scale)
        dkey = jnp.einsum("qhk,qhd->khd", dscores, query_heads).reshape(AUDIO, D)
        dvalue = jnp.einsum("qhk,qhd->khd", probs_low, grad_heads).reshape(AUDIO, D)
        return (carry[0] + dkey, carry[1] + dvalue), None

    start = (jnp.zeros((AUDIO, D), jnp.float32), jnp.zeros((AUDIO, D), jnp.float32))
    sums, unused = lax.scan(video_step, start, (video_query.reshape(blocks, VTOK_DEV, D), video_grad.reshape(blocks, VTOK_DEV, D)))
    dk_audio = rotate(sums[0], audio_pos, -1.0).astype(jnp.bfloat16)
    dv_audio = sums[1].astype(jnp.bfloat16)

    audio_heads = split_heads(audio_query)
    agrad_heads = split_heads(audio_grad)
    key_blocks = video_key.reshape(blocks, VTOK_DEV, D)
    value_blocks = v_video.reshape(blocks, VTOK_DEV, D)
    valid_blocks = video_valid.reshape(blocks, VTOK_DEV)

    def block_scores(key_block, valid_block):
        scores = jnp.einsum("qhd,khd->qhk", audio_heads, split_heads(key_block)) * score_scale
        return jnp.where(valid_block[None, None, :], scores, neg_fill)

    def forward_block(pieces):
        key_block, value_block, valid_block = pieces
        scores = block_scores(key_block, valid_block)
        peak = jnp.max(scores, axis=2)
        raw_weights = jnp.where(valid_block[None, None, :], jnp.exp(scores - peak[:, :, None]), 0.0)
        total = jnp.sum(raw_weights, axis=2)
        numer = jnp.einsum("qhk,khd->qhd", rounded(raw_weights), split_heads(value_block))
        return peak, total, numer

    peaks, totals, numers = lax.map(forward_block, (key_blocks, value_blocks, valid_blocks))
    top = jnp.max(peaks, axis=0)
    factor = jnp.exp(peaks - top[None])
    total_all = jnp.sum(totals * factor, axis=0)
    numer_all = jnp.sum(numers * factor[:, :, :, None], axis=0)
    outputs = numer_all / total_all[:, :, None]
    log_total = top + jnp.log(total_all)
    delta_audio = jnp.sum(agrad_heads * outputs, axis=2)

    def backward_block(pieces):
        key_block, value_block, valid_block = pieces
        scores = block_scores(key_block, valid_block)
        probs = jnp.where(valid_block[None, None, :], jnp.exp(scores - log_total[:, :, None]), 0.0)
        probs_low = rounded(probs)
        dvalue = jnp.einsum("qhk,qhd->khd", probs_low, agrad_heads).reshape(VTOK_DEV, D)
        dprobs = jnp.einsum("qhd,khd->qhk", agrad_heads, split_heads(value_block))
        dscores = rounded(probs * (dprobs - delta_audio[:, :, None]) * score_scale)
        dkey = jnp.einsum("qhk,qhd->khd", dscores, audio_heads).reshape(VTOK_DEV, D)
        return dkey, dvalue

    dkeys, dvalues = lax.map(backward_block, (key_blocks, value_blocks, valid_blocks))
    dk_video = rotate(dkeys.reshape(VIDEO, D), video_pos, -1.0).astype(jnp.bfloat16)
    dv_video = dvalues.reshape(VIDEO, D).astype(jnp.bfloat16)
    return (dk_video, dv_video, dk_audio, dv_audio)
```

```python
import functools

import jax
import jax.numpy as jnp
from jax import lax
from jax.experimental import pallas as pl
from jax.experimental.pallas import tpu as pltpu
from jax.sharding import Mesh
from jax.sharding import PartitionSpec as P

HD = 128
VFRAME = 512
ROPE_BASE = 10000.0
NEG = -1e30
SCALE = HD ** (-0.5)

NY, NZ, NC = 4, 8, 2
HEADS = 12
GROUPS = 4
HPG = HEADS // GROUPS
GW = HPG * HD
CW = HEADS * HD
VT = 128
AR = 4
CR = NC * AR
ZR = NZ * CR
AUDIO = NY * ZR

ALL = ("dp", "yh", "z", "core", "yl")
Y = ("yh", "yl")
f32 = jnp.float32
bf16 = jnp.bfloat16


def frequencies():
    half = HD // 2
    return ROPE_BASE ** (-(jnp.arange(half, dtype=f32) / half))


def turn_tables(where_at):
    angle = where_at.astype(f32)[:, None] * frequencies()[None, :]
    cosine, sine = jnp.cos(angle), jnp.sin(angle)
    return jnp.concatenate([cosine, cosine], 1), jnp.concatenate([-sine, sine], 1)


def rotate_rows(values, cosine, sine):
    rows = values.shape[0]
    shaped = values.astype(f32).reshape(rows, -1, 2, HD // 2)
    swapped = shaped[:, :, ::-1].reshape(rows, -1, HD)
    shaped = shaped.reshape(rows, -1, HD)
    return (shaped * cosine[:, None, :] + swapped * sine[:, None, :]).reshape(rows, -1)


def shift(x, axis, size, step):
    return lax.ppermute(x, axis, [(i, (i + step) % size) for i in range(size)])


def nt(a, b):
    return lax.dot_general(a, b, (((1,), (1,)), ((), ())), preferred_element_type=f32)


def nn(a, b):
    return lax.dot_general(a, b, (((1,), (0,)), ((), ())), preferred_element_type=f32)


def head(i):
    return slice(i * HD, (i + 1) * HD)


def prepare_kernel(sc, q0, q1, k0, k1, v0, v1, d0, d1, cos, sin, qr, kr, vr, dr):
    limit = sc[3]
    for block, (q, k, v, d) in enumerate(((q0, k0, v0, d0), (q1, k1, v1, d1))):
        rows = slice(block * VT, (block + 1) * VT)
        cosine, sine = cos[block : block + 1, :], sin[block : block + 1, :]
        for i in range(HPG):
            for src, dst in ((q, qr), (k, kr)):
                x = src[:, head(i)].astype(f32)
                dst[rows, head(i)] = (
                    x * cosine + pltpu.roll(x, HD // 2, 1) * sine
                ).astype(bf16)
        vr[rows, :] = v[...]
        token = sc[4 + block] + lax.broadcasted_iota(jnp.int32, (VT, GW), 0)
        dr[rows, :] = jnp.where(token < limit, d[...].astype(f32), 0.0).astype(bf16)


def video_to_audio_kernel(sc, q, d, a0, a1, a2, a3, o0, o1, o2, o3):
    core, y, limit = sc[0], sc[1], sc[2]
    row = lax.broadcasted_iota(jnp.int32, (AUDIO, 2 * VT), 0)
    yy = (row // ZR + y) % NY
    zz = (row // CR) % NZ
    r = row % CR
    cc = jnp.where(r < AR, core, 1 - core)
    own = ((yy // 2 * NZ + zz) * NC + cc) * 2 + yy % 2
    valid = own * AR + r % AR < limit
    for i in range(HPG):
        key = jnp.concatenate([a[:, head(i)] for a in (a0, a1, a2, a3)], 0)
        value = jnp.concatenate([a[:, head(HPG + i)] for a in (a0, a1, a2, a3)], 0)
        query, grad = q[:, head(i)], d[:, head(i)]
        s = jnp.where(valid, nt(key, query) * SCALE, NEG)
        e = jnp.exp(s - jnp.max(s, axis=0, keepdims=True))
        p = e * (1.0 / jnp.sum(e, axis=0, keepdims=True))
        pb = p.astype(bf16)
        dp = nt(value, grad)
        delta = jnp.sum(pb.astype(f32) * dp, axis=0, keepdims=True)
        ds = (p * (dp - delta) * SCALE).astype(bf16)
        dk = nn(ds, query).astype(bf16)
        dv = nn(pb, grad).astype(bf16)
        for n, o in enumerate((o0, o1, o2, o3)):
            o[:, head(i)] = dk[n * ZR : (n + 1) * ZR]
            o[:, head(HPG + i)] = dv[n * ZR : (n + 1) * ZR]


def video_mask(sc):
    row = lax.broadcasted_iota(jnp.int32, (2 * VT, AUDIO), 0)
    token = jnp.where(row < VT, sc[4] + row, sc[5] + row - VT)
    return token < sc[3]


def statistics_kernel(sc, k, v, a0, a1, a2, a3, out):
    g = pl.program_id(0)
    valid = video_mask(sc)
    for i in range(HPG):
        query = jnp.concatenate([a[:, head(i)] for a in (a0, a1, a2, a3)], 0)
        grad = jnp.concatenate([a[:, head(HPG + i)] for a in (a0, a1, a2, a3)], 0)
        s = jnp.where(valid, nt(k[:, head(i)], query) * SCALE, NEG)
        m = jnp.max(s, axis=0, keepdims=True)
        e = jnp.where(valid, jnp.exp(s - m), 0.0)
        c = jnp.sum(e, axis=0, keepdims=True)
        eb = e.astype(bf16).astype(f32)
        t = jnp.sum(eb * nt(v[:, head(i)], grad), axis=0, keepdims=True)
        some = c > 0.0
        safe = jnp.where(some, c, 1.0)
        out[pl.ds(g * HPG + i, 1), :] = jnp.where(some, m + jnp.log(safe), NEG)
        out[pl.ds(HEADS + g * HPG + i, 1), :] = jnp.where(some, t / safe, 0.0)

    @pl.when(g == GROUPS - 1)
    def _():
        out[...] = pltpu.roll(out[...], sc[1] * ZR, 1)


def merge(lses, deltas):
    top = functools.reduce(jnp.maximum, lses)
    weights = [jnp.exp(x - top) for x in lses]
    total = sum(weights)
    delta = sum(w * x for w, x in zip(weights, deltas)) / total
    return top + jnp.log(total), delta


def merge_kernel(sc, *refs, count, back):
    *parts, out = refs
    if count > 1:
        (part,) = parts
        parts = [part.at[n] for n in range(count)]
    lse, delta = merge([p[:HEADS] for p in parts], [p[HEADS:] for p in parts])
    both = jnp.concatenate([lse, delta], 0)
    if back:
        both = pltpu.roll(both, lax.rem(AUDIO - sc[1] * ZR, AUDIO), 1)
    out[...] = both


def audio_to_video_kernel(sc, k, v, stats, cos, sin, a0, a1, a2, a3, dk0, dk1, dv0, dv1):
    g = pl.program_id(0)
    valid = video_mask(sc)
    for i in range(HPG):
        query = jnp.concatenate([a[:, head(i)] for a in (a0, a1, a2, a3)], 0)
        grad = jnp.concatenate([a[:, head(HPG + i)] for a in (a0, a1, a2, a3)], 0)
        lse = stats[pl.ds(g * HPG + i, 1), :]
        delta = stats[pl.ds(HEADS + g * HPG + i, 1), :]
        s = nt(k[:, head(i)], query) * SCALE
        p = jnp.where(valid, jnp.exp(s - lse), 0.0)
        dp = nt(v[:, head(i)], grad)
        ds = (p * (dp - delta) * SCALE).astype(bf16)
        dv = nn(p.astype(bf16), grad)
        dk = nn(ds, query)
        for block, (dko, dvo) in enumerate(((dk0, dv0), (dk1, dv1))):
            rows = slice(block * VT, (block + 1) * VT)
            x = dk[rows]
            dko[:, head(i)] = (
                x * cos[block : block + 1, :]
                - pltpu.roll(x, HD // 2, 1) * sin[block : block + 1, :]
            ).astype(bf16)
            dvo[:, head(i)] = dv[rows].astype(bf16)


def call(kernel, scalars, args, specs, outs, out_specs, grid=(GROUPS,), flops=0):
    size = sum(x.size * x.dtype.itemsize for x in args)
    return pl.pallas_call(
        kernel,
        grid_spec=pltpu.PrefetchScalarGridSpec(
            num_scalar_prefetch=1, grid=grid, in_specs=specs, out_specs=out_specs
        ),
        out_shape=outs,
        compiler_params=pltpu.CompilerParams(vmem_limit_bytes=40 * 1024 * 1024),
        cost_estimate=pl.CostEstimate(flops=flops, bytes_accessed=size, transcendentals=0),
    )(scalars, *args)


def local(q_video, k_video, v_video, d_video, q_audio, k_audio, v_audio, d_audio, audio_pos, video_len, audio_len):
    yh, z, core, yl = (lax.axis_index(a) for a in ("yh", "z", "core", "yl"))
    y = yh * 2 + yl
    own = ((yh * NZ + z) * NC + core) * 2 + yl
    pair = ((yh * NZ + z) * NC + 1 - core) * 2 + yl
    scalars = jnp.stack(
        [core, y, audio_len[0], video_len[0], own * VT, pair * VT]
    ).astype(jnp.int32)
    first = core == 0

    audio_cos, audio_sin = turn_tables(audio_pos)
    ours = own * AR + jnp.arange(AR, dtype=jnp.int32) < audio_len[0]
    q_rot = rotate_rows(q_audio, audio_cos, audio_sin).astype(bf16)
    k_rot = rotate_rows(k_audio, audio_cos, audio_sin).astype(bf16)
    d_own = jnp.where(ours[:, None], d_audio, jnp.zeros_like(d_audio))

    def packed(a, b):
        a = a.reshape(AR, NC, GROUPS, 1, GW)
        b = b.reshape(AR, NC, GROUPS, 1, GW)
        both = jnp.concatenate([a, b], 3).reshape(AR, NC, 2 * CW)
        keep = jnp.where(first, both[:, 0], both[:, 1])
        give = jnp.where(first, both[:, 1], both[:, 0])
        return keep, give

    keep_kv, give_kv = packed(k_rot, v_audio)
    keep_qd, give_qd = packed(q_rot, d_own)
    kv = jnp.concatenate([keep_kv, shift(give_kv, "core", NC, 1)], 0)
    qd = jnp.concatenate([keep_qd, shift(give_qd, "core", NC, 1)], 0)

    def along_z(x):
        copies = jnp.broadcast_to(x[None], (NZ,) + x.shape).reshape(ZR, 2 * CW)
        return lax.all_to_all(copies, "z", split_axis=0, concat_axis=0, tiled=True)

    def along_y(x):
        return [x] + [shift(x, Y, NY, NY - n) for n in range(1, NY)]

    kv_all = along_y(along_z(kv))
    qd_all = along_y(along_z(qd))

    q_pair, k_pair, v_pair, d_pair = (
        shift(x, "core", NC, 1) for x in (q_video, k_video, v_video, d_video)
    )
    cos, sin = turn_tables(jnp.stack([own * VT // VFRAME, pair * VT // VFRAME]))
    half = pl.BlockSpec((VT, GW), lambda g, sc: (0, sc[0] * GROUPS + g))
    table = pl.BlockSpec((2, HD), lambda g, sc: (0, 0))
    video = pl.BlockSpec((2 * VT, GW), lambda g, sc: (0, g))
    audio = pl.BlockSpec((ZR, 2 * GW), lambda g, sc: (0, g))
    rows = pl.BlockSpec((2 * HEADS, AUDIO), lambda g, sc: (0, 0))
    mine = pl.BlockSpec((VT, GW), lambda g, sc: (0, g))
    video_shape = jax.ShapeDtypeStruct((2 * VT, CW), bf16)
    rows_shape = jax.ShapeDtypeStruct((2 * HEADS, AUDIO), f32)
    mine_shape = jax.ShapeDtypeStruct((VT, CW), bf16)
    audio_shape = jax.ShapeDtypeStruct((ZR, 2 * CW), bf16)
    one = 2 * 2 * VT * AUDIO * CW

    qr, kr, vr, dr = call(
        prepare_kernel,
        scalars,
        (q_video, q_pair, k_video, k_pair, v_video, v_pair, d_video, d_pair, cos, sin),
        [half] * 8 + [table] * 2,
        [video_shape] * 4,
        [video] * 4,
    )

    parts = call(
        video_to_audio_kernel,
        scalars,
        (qr, dr, *kv_all),
        [video] * 2 + [audio] * NY,
        [audio_shape] * NY,
        [audio] * NY,
        flops=4 * one,
    )
    sums = parts[0].astype(f32)
    for n in range(1, NY):
        sums = sums + shift(parts[n], Y, NY, n).astype(f32)
    sums = lax.all_to_all(sums.astype(bf16), "z", split_axis=0, concat_axis=0, tiled=True)
    sums = jnp.sum(sums.reshape(NZ, CR, 2 * CW).astype(f32), 0)
    other = shift(sums[AR:], "core", NC, 1)
    sums = sums[:AR]
    sums = jnp.stack([jnp.where(first, sums, other), jnp.where(first, other, sums)], 1)
    sums = sums.reshape(AR, NC, GROUPS, 2, GW)
    dk_sum = sums[:, :, :, 0].reshape(AR, NC * CW)
    dk_audio = rotate_rows(dk_sum, audio_cos, -audio_sin).astype(bf16)
    dv_audio = sums[:, :, :, 1].reshape(AR, NC * CW).astype(bf16)

    stats = call(
        statistics_kernel,
        scalars,
        (kr, vr, *qd_all),
        [video] * 2 + [audio] * NY,
        rows_shape,
        rows,
        flops=2 * one,
    )
    stats = call(
        functools.partial(merge_kernel, count=1, back=False),
        scalars,
        along_y(stats),
        [rows] * NY,
        rows_shape,
        rows,
        grid=(1,),
    )
    copies = jnp.broadcast_to(stats[None], (NZ,) + stats.shape)
    stats = lax.all_to_all(copies, "z", split_axis=0, concat_axis=0, tiled=True)
    stats = call(
        functools.partial(merge_kernel, count=NZ, back=True),
        scalars,
        (stats,),
        [pl.BlockSpec(stats.shape, lambda g, sc: (0, 0, 0))],
        rows_shape,
        rows,
        grid=(1,),
    )
    dk0, dk1, dv0, dv1 = call(
        audio_to_video_kernel,
        scalars,
        (kr, vr, stats, cos, sin, *qd_all),
        [video] * 2 + [rows] + [table] * 2 + [audio] * NY,
        [mine_shape] * 4,
        [mine] * 4,
        flops=4 * one,
    )

    def joined(a, b):
        b = shift(b, "core", NC, 1)
        return jnp.concatenate([jnp.where(first, a, b), jnp.where(first, b, a)], 1)

    return joined(dk0, dk1), joined(dv0, dv1), dk_audio, dv_audio


def solution(mesh):
    fine = Mesh(mesh.devices.reshape(mesh.shape["dp"], 2, NZ, NC, 2), ALL)
    rows = P(ALL, None)
    return jax.shard_map(
        local,
        mesh=fine,
        in_specs=(rows,) * 8 + (P(ALL), P("dp"), P("dp")),
        out_specs=(rows,) * 4,
        check_vma=False,
    )
```

```python
import functools

import jax
import jax.numpy as jnp
import numpy as np
from jax import lax
from jax.experimental import pallas as pl
from jax.experimental.pallas import tpu as pltpu
from jax.sharding import Mesh
from jax.sharding import PartitionSpec as P

HD = 128
VFRAME = 512
ROPE_BASE = 10000.0
NEG = -1e30
SCALE = HD ** (-0.5)

NY, NZ, NC = 4, 8, 2
HEADS = 12
GROUPS = 4
HPG = HEADS // GROUPS
GW = HPG * HD
CW = HEADS * HD
VT = 128
AR = 4
CR = NC * AR
ZR = NZ * CR
YR = NY * CR
AUDIO = NY * ZR

ALL = ("dp", "yh", "z", "core", "yl")
Y = ("yh", "yl")
f32 = jnp.float32
bf16 = jnp.bfloat16


def frequencies():
    half = HD // 2
    return ROPE_BASE ** (-(jnp.arange(half, dtype=f32) / half))


def turn_tables(where_at):
    angle = where_at.astype(f32)[:, None] * frequencies()[None, :]
    cosine, sine = jnp.cos(angle), jnp.sin(angle)
    return jnp.concatenate([cosine, cosine], 1), jnp.concatenate([-sine, sine], 1)


def rotate_rows(values, cosine, sine):
    rows = values.shape[0]
    shaped = values.astype(f32).reshape(rows, -1, 2, HD // 2)
    swapped = shaped[:, :, ::-1].reshape(rows, -1, HD)
    shaped = shaped.reshape(rows, -1, HD)
    return (shaped * cosine[:, None, :] + swapped * sine[:, None, :]).reshape(rows, -1)


def shift(x, axis, size, step):
    return lax.ppermute(x, axis, [(i, (i + step) % size) for i in range(size)])


def nt(a, b):
    return lax.dot_general(a, b, (((1,), (1,)), ((), ())), preferred_element_type=f32)


def nn(a, b):
    return lax.dot_general(a, b, (((1,), (0,)), ((), ())), preferred_element_type=f32)


def head(i):
    return slice(i * HD, (i + 1) * HD)


def prepare_kernel(sc, q0, q1, k0, k1, v0, v1, d0, d1, cos, sin, qr, kr, vr, dr):
    limit = sc[3]
    for block, (q, k, v, d) in enumerate(((q0, k0, v0, d0), (q1, k1, v1, d1))):
        rows = slice(block * VT, (block + 1) * VT)
        cosine, sine = cos[block : block + 1, :], sin[block : block + 1, :]
        for i in range(HPG):
            for src, dst in ((q, qr), (k, kr)):
                x = src[:, head(i)].astype(f32)
                dst[rows, head(i)] = (
                    x * cosine + pltpu.roll(x, HD // 2, 1) * sine
                ).astype(bf16)
        vr[rows, :] = v[...]
        token = sc[4 + block] + lax.broadcasted_iota(jnp.int32, (VT, GW), 0)
        dr[rows, :] = jnp.where(token < limit, d[...].astype(f32), 0.0).astype(bf16)


def video_to_audio_kernel(sc, q, d, *refs):
    blocks, outs = refs[:-NY], refs[-NY:]
    core, y, limit, z = sc[0], sc[1], sc[2], sc[6]
    row = lax.broadcasted_iota(jnp.int32, (AUDIO, 2 * VT), 0)
    zz = (row // YR + z) % NZ
    yy = (row // CR + y) % NY
    r = row % CR
    cc = jnp.where(r < AR, core, 1 - core)
    own = ((yy // 2 * NZ + zz) * NC + cc) * 2 + yy % 2
    valid = own * AR + r % AR < limit
    for i in range(HPG):
        key = jnp.concatenate([a[:, head(i)] for a in blocks], 0)
        value = jnp.concatenate([a[:, head(HPG + i)] for a in blocks], 0)
        query, grad = q[:, head(i)], d[:, head(i)]
        s = jnp.where(valid, nt(key, query) * SCALE, NEG)
        e = jnp.exp(s - jnp.max(s, axis=0, keepdims=True))
        p = e * (1.0 / jnp.sum(e, axis=0, keepdims=True))
        pb = p.astype(bf16)
        dp = nt(value, grad)
        delta = jnp.sum(pb.astype(f32) * dp, axis=0, keepdims=True)
        ds = (p * (dp - delta) * SCALE).astype(bf16)
        dk = nn(ds, query).reshape(NZ, NY, CR, HD)
        dv = nn(pb, grad).reshape(NZ, NY, CR, HD)
        for n, o in enumerate(outs):
            o[:, head(i)] = dk[:, n].reshape(ZR, HD).astype(bf16)
            o[:, head(HPG + i)] = dv[:, n].reshape(ZR, HD).astype(bf16)


def sum_kernel(sc, p0, p1, p2, p3, out, twice):
    total = sum(p[...].astype(f32) for p in (p0, p1, p2, p3))
    twice[:ZR, :] = total
    twice[ZR:, :] = total
    start = pl.multiple_of(lax.rem(NZ - sc[6], NZ) * CR, CR)
    out[...] = twice[pl.ds(start, ZR), :].astype(bf16)


def audio_kernel(sc, q, k, v, d, freq, keep, give):
    core, own = sc[0], sc[7]
    row = lax.broadcasted_iota(jnp.int32, (AR, HD), 0)
    lane = lax.broadcasted_iota(jnp.int32, (AR, HD), 1)
    pos = functools.reduce(lambda a, n: jnp.where(row == n, sc[8 + n], a), range(1, AR), sc[8])
    angle = pos.astype(f32) * freq[...]
    cosine = jnp.cos(angle)
    sine = jnp.where(lane < HD // 2, -jnp.sin(angle), jnp.sin(angle))
    ours = own * AR + row < sc[2]

    def turn(x):
        x = x.astype(f32)
        swapped = jnp.concatenate([x[:, HD // 2 :], x[:, : HD // 2]], 1)
        return x * cosine + swapped * sine

    def pair(ref, n, change):
        return [change(ref[:, head(c * HEADS + n)]) for c in range(NC)]

    same = lambda x: x.astype(f32)
    clear = lambda x: jnp.where(ours, x.astype(f32), 0.0)
    for n in range(HEADS):
        base = n // HPG * 2 * GW + n % HPG * HD
        for at, ref, change in ((0, k, turn), (GW, v, same), (2 * CW, q, turn), (2 * CW + GW, d, clear)):
            a, b = pair(ref, n, change)
            lanes = slice(base + at, base + at + HD)
            keep[:, lanes] = jnp.where(core == 0, a, b).astype(bf16)
            give[:, lanes] = jnp.where(core == 0, b, a).astype(bf16)


def video_mask(sc):
    row = lax.broadcasted_iota(jnp.int32, (2 * VT, AUDIO), 0)
    token = jnp.where(row < VT, sc[4] + row, sc[5] + row - VT)
    return token < sc[3]


def statistics_kernel(sc, k, v, a0, a1, a2, a3, out):
    g = pl.program_id(0)
    valid = video_mask(sc)
    for i in range(HPG):
        query = jnp.concatenate([a[:, head(i)] for a in (a0, a1, a2, a3)], 0)
        grad = jnp.concatenate([a[:, head(HPG + i)] for a in (a0, a1, a2, a3)], 0)
        s = jnp.where(valid, nt(k[:, head(i)], query) * SCALE, NEG)
        m = jnp.max(s, axis=0, keepdims=True)
        e = jnp.where(valid, jnp.exp(s - m), 0.0)
        c = jnp.sum(e, axis=0, keepdims=True)
        eb = e.astype(bf16).astype(f32)
        t = jnp.sum(eb * nt(v[:, head(i)], grad), axis=0, keepdims=True)
        some = c > 0.0
        safe = jnp.where(some, c, 1.0)
        out[pl.ds(g * HPG + i, 1), :] = jnp.where(some, m + jnp.log(safe), NEG)
        out[pl.ds(HEADS + g * HPG + i, 1), :] = jnp.where(some, t / safe, 0.0)

    @pl.when(g == GROUPS - 1)
    def _():
        out[...] = pltpu.roll(out[...], sc[1] * ZR, 1)


def merge(lses, deltas):
    top = functools.reduce(jnp.maximum, lses)
    weights = [jnp.exp(x - top) for x in lses]
    total = sum(weights)
    delta = sum(w * x for w, x in zip(weights, deltas)) / total
    return top + jnp.log(total), delta


def merge_kernel(sc, *refs, count, back):
    *parts, out = refs
    if count > 1:
        (part,) = parts
        parts = [part.at[n] for n in range(count)]
    lse, delta = merge([p[:HEADS] for p in parts], [p[HEADS:] for p in parts])
    both = jnp.concatenate([lse, delta], 0)
    if back:
        both = pltpu.roll(both, lax.rem(AUDIO - sc[1] * ZR, AUDIO), 1)
    out[...] = both


def audio_to_video_kernel(sc, k, v, stats, cos, sin, a0, a1, a2, a3, dk0, dk1, dv0, dv1):
    g = pl.program_id(0)
    valid = video_mask(sc)
    for i in range(HPG):
        query = jnp.concatenate([a[:, head(i)] for a in (a0, a1, a2, a3)], 0)
        grad = jnp.concatenate([a[:, head(HPG + i)] for a in (a0, a1, a2, a3)], 0)
        lse = stats[pl.ds(g * HPG + i, 1), :]
        delta = stats[pl.ds(HEADS + g * HPG + i, 1), :]
        s = nt(k[:, head(i)], query) * SCALE
        p = jnp.where(valid, jnp.exp(s - lse), 0.0)
        dp = nt(v[:, head(i)], grad)
        ds = (p * (dp - delta) * SCALE).astype(bf16)
        dv = nn(p.astype(bf16), grad)
        dk = nn(ds, query)
        for block, (dko, dvo) in enumerate(((dk0, dv0), (dk1, dv1))):
            rows = slice(block * VT, (block + 1) * VT)
            x = dk[rows]
            dko[:, head(i)] = (
                x * cos[block : block + 1, :]
                - pltpu.roll(x, HD // 2, 1) * sin[block : block + 1, :]
            ).astype(bf16)
            dvo[:, head(i)] = dv[rows].astype(bf16)


def call(kernel, scalars, args, specs, outs, out_specs, grid=(GROUPS,), flops=0, scratch=()):
    size = sum(x.size * x.dtype.itemsize for x in args)
    return pl.pallas_call(
        kernel,
        grid_spec=pltpu.PrefetchScalarGridSpec(
            num_scalar_prefetch=1, grid=grid, in_specs=specs, out_specs=out_specs, scratch_shapes=scratch
        ),
        out_shape=outs,
        compiler_params=pltpu.CompilerParams(vmem_limit_bytes=16 * 1024 * 1024),
        cost_estimate=pl.CostEstimate(flops=flops, bytes_accessed=size, transcendentals=0),
    )(scalars, *args)


def local(q_video, k_video, v_video, d_video, q_audio, k_audio, v_audio, d_audio, audio_pos, video_len, audio_len):
    yh, z, core, yl = (lax.axis_index(a) for a in ("yh", "z", "core", "yl"))
    y = yh * 2 + yl
    own = ((yh * NZ + z) * NC + core) * 2 + yl
    pair = ((yh * NZ + z) * NC + 1 - core) * 2 + yl
    scalars = jnp.stack(
        [core, y, audio_len[0], video_len[0], own * VT, pair * VT, z, own, *audio_pos]
    ).astype(jnp.int32)
    first = core == 0

    audio_cos, audio_sin = turn_tables(audio_pos)

    frequency = np.tile(ROPE_BASE ** (-np.arange(HD // 2) / (HD // 2)), 2).astype(np.float32)
    whole = pl.BlockSpec((AR, NC * CW), lambda g, sc: (0, 0))
    wide = pl.BlockSpec((AR, 4 * CW), lambda g, sc: (0, 0))
    keep, give = call(
        audio_kernel,
        scalars,
        (q_audio, k_audio, v_audio, d_audio, frequency[None]),
        [whole] * 4 + [pl.BlockSpec((1, HD), lambda g, sc: (0, 0))],
        [jax.ShapeDtypeStruct((AR, 4 * CW), bf16)] * 2,
        [wide] * 2,
        grid=(1,),
    )
    chip = jnp.concatenate([keep, shift(give, "core", NC, 1)], 0)
    kv, qd = chip[:, : 2 * CW], chip[:, 2 * CW :]

    def along_y(x):
        return [x] + [shift(x, Y, NY, NY - n) for n in range(1, NY)]

    home = jnp.concatenate(along_y(kv), 0)
    up, down = [home], [home]
    for _ in range(3):
        up.append(shift(up[-1], "z", NZ, NZ - 1))
        down.append(shift(down[-1], "z", NZ, 1))
    far = [shift(up[-1][: YR // 2], "z", NZ, NZ - 1), shift(down[-1][YR // 2 :], "z", NZ, 1)]
    kv_all = up + far + down[:0:-1]

    copies = jnp.broadcast_to(qd[None], (NZ,) + qd.shape).reshape(ZR, 2 * CW)
    qd_all = along_y(lax.all_to_all(copies, "z", split_axis=0, concat_axis=0, tiled=True))

    q_pair, k_pair, v_pair, d_pair = (
        shift(x, "core", NC, 1) for x in (q_video, k_video, v_video, d_video)
    )
    cos, sin = turn_tables(jnp.stack([own * VT // VFRAME, pair * VT // VFRAME]))
    half = pl.BlockSpec((VT, GW), lambda g, sc: (0, sc[0] * GROUPS + g))
    table = pl.BlockSpec((2, HD), lambda g, sc: (0, 0))
    video = pl.BlockSpec((2 * VT, GW), lambda g, sc: (0, g))
    audio = pl.BlockSpec((ZR, 2 * GW), lambda g, sc: (0, g))
    rows = pl.BlockSpec((2 * HEADS, AUDIO), lambda g, sc: (0, 0))
    mine = pl.BlockSpec((VT, GW), lambda g, sc: (0, g))
    video_shape = jax.ShapeDtypeStruct((2 * VT, CW), bf16)
    rows_shape = jax.ShapeDtypeStruct((2 * HEADS, AUDIO), f32)
    mine_shape = jax.ShapeDtypeStruct((VT, CW), bf16)
    audio_shape = jax.ShapeDtypeStruct((ZR, 2 * CW), bf16)
    one = 2 * 2 * VT * AUDIO * CW

    qr, kr, vr, dr = call(
        prepare_kernel,
        scalars,
        (q_video, q_pair, k_video, k_pair, v_video, v_pair, d_video, d_pair, cos, sin),
        [half] * 8 + [table] * 2,
        [video_shape] * 4,
        [video] * 4,
    )

    parts = call(
        video_to_audio_kernel,
        scalars,
        (qr, dr, *kv_all),
        [video] * 2 + [pl.BlockSpec((x.shape[0], 2 * GW), lambda g, sc: (0, g)) for x in kv_all],
        [audio_shape] * NY,
        [audio] * NY,
        flops=4 * one,
    )
    sums = call(
        sum_kernel,
        scalars,
        [parts[0]] + [shift(parts[n], Y, NY, n) for n in range(1, NY)],
        [audio] * NY,
        audio_shape,
        audio,
        scratch=[pltpu.VMEM((2 * ZR, 2 * GW), f32)],
    )
    sums = lax.all_to_all(sums, "z", split_axis=0, concat_axis=0, tiled=True)
    sums = jnp.sum(sums.reshape(NZ, CR, 2 * CW).astype(f32), 0)
    other = shift(sums[AR:], "core", NC, 1)
    sums = sums[:AR]
    sums = jnp.stack([jnp.where(first, sums, other), jnp.where(first, other, sums)], 1)
    sums = sums.reshape(AR, NC, GROUPS, 2, GW)
    dk_sum = sums[:, :, :, 0].reshape(AR, NC * CW)
    dk_audio = rotate_rows(dk_sum, audio_cos, -audio_sin).astype(bf16)
    dv_audio = sums[:, :, :, 1].reshape(AR, NC * CW).astype(bf16)

    stats = call(
        statistics_kernel,
        scalars,
        (kr, vr, *qd_all),
        [video] * 2 + [audio] * NY,
        rows_shape,
        rows,
        flops=2 * one,
    )
    stats = call(
        functools.partial(merge_kernel, count=1, back=False),
        scalars,
        along_y(stats),
        [rows] * NY,
        rows_shape,
        rows,
        grid=(1,),
    )
    copies = jnp.broadcast_to(stats[None], (NZ,) + stats.shape)
    stats = lax.all_to_all(copies, "z", split_axis=0, concat_axis=0, tiled=True)
    stats = call(
        functools.partial(merge_kernel, count=NZ, back=True),
        scalars,
        (stats,),
        [pl.BlockSpec(stats.shape, lambda g, sc: (0, 0, 0))],
        rows_shape,
        rows,
        grid=(1,),
    )
    dk0, dk1, dv0, dv1 = call(
        audio_to_video_kernel,
        scalars,
        (kr, vr, stats, cos, sin, *qd_all),
        [video] * 2 + [rows] + [table] * 2 + [audio] * NY,
        [mine_shape] * 4,
        [mine] * 4,
        flops=4 * one,
    )

    def joined(a, b):
        b = shift(b, "core", NC, 1)
        return jnp.concatenate([jnp.where(first, a, b), jnp.where(first, b, a)], 1)

    return joined(dk0, dk1), joined(dv0, dv1), dk_audio, dv_audio


def solution(mesh):
    fine = Mesh(mesh.devices.reshape(mesh.shape["dp"], 2, NZ, NC, 2), ALL)
    rows = P(ALL, None)
    return jax.shard_map(
        local,
        mesh=fine,
        in_specs=(rows,) * 8 + (P(ALL), P("dp"), P("dp")),
        out_specs=(rows,) * 4,
        check_vma=False,
    )
```

```python
import functools

import jax
import jax.numpy as jnp
import numpy as np
from jax import lax
from jax.experimental import pallas as pl
from jax.experimental.pallas import tpu as pltpu
from jax.sharding import Mesh
from jax.sharding import PartitionSpec as P

HD = 128
VFRAME = 512
ROPE_BASE = 10000.0
NEG = -1e30
SCALE = HD ** (-0.5)

NY, NZ, NC = 4, 8, 2
HEADS = 12
GROUPS = 2
HPG = HEADS // GROUPS
GW = HPG * HD
CW = HEADS * HD
VT = 128
AR = 4
CR = NC * AR
ZR = NZ * CR
YR = NY * CR
AUDIO = NY * ZR

ALL = ("dp", "yh", "z", "core", "yl")
Y = ("yh", "yl")
f32 = jnp.float32
bf16 = jnp.bfloat16


def frequencies():
    half = HD // 2
    return ROPE_BASE ** (-(jnp.arange(half, dtype=f32) / half))


def turn_tables(where_at):
    angle = where_at.astype(f32)[:, None] * frequencies()[None, :]
    cosine, sine = jnp.cos(angle), jnp.sin(angle)
    return jnp.concatenate([cosine, cosine], 1), jnp.concatenate([-sine, sine], 1)


def rotate_rows(values, cosine, sine):
    rows = values.shape[0]
    shaped = values.astype(f32).reshape(rows, -1, 2, HD // 2)
    swapped = shaped[:, :, ::-1].reshape(rows, -1, HD)
    shaped = shaped.reshape(rows, -1, HD)
    return (shaped * cosine[:, None, :] + swapped * sine[:, None, :]).reshape(rows, -1)


def shift(x, axis, size, step):
    return lax.ppermute(x, axis, [(i, (i + step) % size) for i in range(size)])


def nt(a, b):
    return lax.dot_general(a, b, (((1,), (1,)), ((), ())), preferred_element_type=f32)


def nn(a, b):
    return lax.dot_general(a, b, (((1,), (0,)), ((), ())), preferred_element_type=f32)


def head(i):
    return slice(i * HD, (i + 1) * HD)


def prepare_kernel(sc, q0, q1, k0, k1, v0, v1, d0, d1, cos, sin, qr, kr, vr, dr):
    limit = sc[3]
    for block, (q, k, v, d) in enumerate(((q0, k0, v0, d0), (q1, k1, v1, d1))):
        rows = slice(block * VT, (block + 1) * VT)
        cosine, sine = cos[block : block + 1, :], sin[block : block + 1, :]
        for i in range(HPG):
            for src, dst in ((q, qr), (k, kr)):
                x = src[:, head(i)].astype(f32)
                dst[rows, head(i)] = (
                    x * cosine + pltpu.roll(x, HD // 2, 1) * sine
                ).astype(bf16)
        vr[rows, :] = v[...]
        token = sc[4 + block] + lax.broadcasted_iota(jnp.int32, (VT, GW), 0)
        dr[rows, :] = jnp.where(token < limit, d[...].astype(f32), 0.0).astype(bf16)


def video_to_audio_kernel(sc, q, d, *refs):
    blocks, outs = refs[:-NY], refs[-NY:]
    core, y, limit, z = sc[0], sc[1], sc[2], sc[6]
    row = lax.broadcasted_iota(jnp.int32, (AUDIO, 2 * VT), 0)
    zz = (row // YR + z) % NZ
    yy = (row // CR + y) % NY
    r = row % CR
    cc = jnp.where(r < AR, core, 1 - core)
    own = ((yy // 2 * NZ + zz) * NC + cc) * 2 + yy % 2
    valid = own * AR + r % AR < limit
    for i in range(HPG):
        key = jnp.concatenate([a[:, head(i)] for a in blocks], 0)
        value = jnp.concatenate([a[:, head(HPG + i)] for a in blocks], 0)
        query, grad = q[:, head(i)], d[:, head(i)]
        s = jnp.where(valid, nt(key, query) * SCALE, NEG)
        e = jnp.exp(s - jnp.max(s, axis=0, keepdims=True))
        p = e * (1.0 / jnp.sum(e, axis=0, keepdims=True))
        pb = p.astype(bf16)
        dp = nt(value, grad)
        delta = jnp.sum(pb.astype(f32) * dp, axis=0, keepdims=True)
        ds = (p * (dp - delta) * SCALE).astype(bf16)
        dk = nn(ds, query).reshape(NZ, NY, CR, HD)
        dv = nn(pb, grad).reshape(NZ, NY, CR, HD)
        for n, o in enumerate(outs):
            o[:, head(i)] = dk[:, n].reshape(ZR, HD).astype(bf16)
            o[:, head(HPG + i)] = dv[:, n].reshape(ZR, HD).astype(bf16)


def sum_kernel(sc, p0, p1, p2, p3, out, twice):
    total = sum(p[...].astype(f32) for p in (p0, p1, p2, p3))
    twice[:ZR, :] = total
    twice[ZR:, :] = total
    start = pl.multiple_of(lax.rem(NZ - sc[6], NZ) * CR, CR)
    out[...] = twice[pl.ds(start, ZR), :].astype(bf16)


def audio_kernel(sc, q, k, v, d, freq, keep, give):
    core, own = sc[0], sc[7]
    row = lax.broadcasted_iota(jnp.int32, (AR, HD), 0)
    lane = lax.broadcasted_iota(jnp.int32, (AR, HD), 1)
    pos = functools.reduce(lambda a, n: jnp.where(row == n, sc[8 + n], a), range(1, AR), sc[8])
    angle = pos.astype(f32) * freq[...]
    cosine = jnp.cos(angle)
    sine = jnp.where(lane < HD // 2, -jnp.sin(angle), jnp.sin(angle))
    ours = own * AR + row < sc[2]

    def turn(x):
        x = x.astype(f32)
        swapped = jnp.concatenate([x[:, HD // 2 :], x[:, : HD // 2]], 1)
        return x * cosine + swapped * sine

    def pair(ref, n, change):
        return [change(ref[:, head(c * HEADS + n)]) for c in range(NC)]

    same = lambda x: x.astype(f32)
    clear = lambda x: jnp.where(ours, x.astype(f32), 0.0)
    for n in range(HEADS):
        base = n // HPG * 2 * GW + n % HPG * HD
        for at, ref, change in ((base, k, turn), (base + GW, v, same), (2 * CW + base, q, turn), (2 * CW + base + GW, d, clear)):
            a, b = pair(ref, n, change)
            lanes = slice(at, at + HD)
            keep[:, lanes] = jnp.where(core == 0, a, b).astype(bf16)
            give[:, lanes] = jnp.where(core == 0, b, a).astype(bf16)


def video_mask(sc):
    row = lax.broadcasted_iota(jnp.int32, (2 * VT, AUDIO), 0)
    token = jnp.where(row < VT, sc[4] + row, sc[5] + row - VT)
    return token < sc[3]


def statistics_kernel(sc, k, v, a0, a1, a2, a3, out):
    g = pl.program_id(0)
    valid = video_mask(sc)
    for i in range(HPG):
        query = jnp.concatenate([a[:, head(i)] for a in (a0, a1, a2, a3)], 0)
        grad = jnp.concatenate([a[:, head(HPG + i)] for a in (a0, a1, a2, a3)], 0)
        s = jnp.where(valid, nt(k[:, head(i)], query) * SCALE, NEG)
        m = jnp.max(s, axis=0, keepdims=True)
        e = jnp.where(valid, jnp.exp(s - m), 0.0)
        c = jnp.sum(e, axis=0, keepdims=True)
        eb = e.astype(bf16).astype(f32)
        t = jnp.sum(eb * nt(v[:, head(i)], grad), axis=0, keepdims=True)
        some = c > 0.0
        safe = jnp.where(some, c, 1.0)
        out[pl.ds(g * HPG + i, 1), :] = jnp.where(some, m + jnp.log(safe), NEG)
        out[pl.ds(HEADS + g * HPG + i, 1), :] = jnp.where(some, t / safe, 0.0)


def merge(lses, deltas):
    top = functools.reduce(jnp.maximum, lses)
    weights = [jnp.exp(x - top) for x in lses]
    total = sum(weights)
    delta = sum(w * x for w, x in zip(weights, deltas)) / total
    return top + jnp.log(total), delta


def merge_kernel(sc, *refs, count, turn):
    *parts, out = refs
    if count > 1:
        (part,) = parts
        parts = [part.at[n] for n in range(count)]
    lse, delta = merge([p[:HEADS] for p in parts], [p[HEADS:] for p in parts])
    both = jnp.concatenate([lse, delta], 0)
    out[...] = pltpu.roll(both, lax.rem(AUDIO + turn * sc[1] * ZR, AUDIO), 1)


def audio_to_video_kernel(sc, k, v, stats, cos, sin, a0, a1, a2, a3, dk0, dk1, dv0, dv1):
    g = pl.program_id(0)
    valid = video_mask(sc)
    for i in range(HPG):
        query = jnp.concatenate([a[:, head(i)] for a in (a0, a1, a2, a3)], 0)
        grad = jnp.concatenate([a[:, head(HPG + i)] for a in (a0, a1, a2, a3)], 0)
        lse = stats[pl.ds(g * HPG + i, 1), :]
        delta = stats[pl.ds(HEADS + g * HPG + i, 1), :]
        s = nt(k[:, head(i)], query) * SCALE
        p = jnp.where(valid, jnp.exp(s - lse), 0.0)
        dp = nt(v[:, head(i)], grad)
        ds = (p * (dp - delta) * SCALE).astype(bf16)
        dv = nn(p.astype(bf16), grad)
        dk = nn(ds, query)
        for block, (dko, dvo) in enumerate(((dk0, dv0), (dk1, dv1))):
            rows = slice(block * VT, (block + 1) * VT)
            x = dk[rows]
            dko[:, head(i)] = (
                x * cos[block : block + 1, :]
                - pltpu.roll(x, HD // 2, 1) * sin[block : block + 1, :]
            ).astype(bf16)
            dvo[:, head(i)] = dv[rows].astype(bf16)


def join_kernel(sc, k0, k1, v0, v1, dk, dv):
    for a, b, out in ((k0, k1, dk), (v0, v1, dv)):

        @pl.when(sc[0] == 0)
        def _():
            out[:, :CW] = a[...]
            out[:, CW:] = b[...]

        @pl.when(sc[0] != 0)
        def _():
            out[:, :CW] = b[...]
            out[:, CW:] = a[...]


def call(kernel, scalars, args, specs, outs, out_specs, grid=(GROUPS,), flops=0, limit=56, scratch=()):
    size = sum(x.size * x.dtype.itemsize for x in args)
    return pl.pallas_call(
        kernel,
        grid_spec=pltpu.PrefetchScalarGridSpec(
            num_scalar_prefetch=1, grid=grid, in_specs=specs, out_specs=out_specs, scratch_shapes=scratch
        ),
        out_shape=outs,
        compiler_params=pltpu.CompilerParams(vmem_limit_bytes=limit * 1024 * 1024),
        cost_estimate=pl.CostEstimate(flops=0, bytes_accessed=0, transcendentals=0),
    )(scalars, *args)


def local(q_video, k_video, v_video, d_video, q_audio, k_audio, v_audio, d_audio, audio_pos, video_len, audio_len):
    yh, z, core, yl = (lax.axis_index(a) for a in ("yh", "z", "core", "yl"))
    y = yh * 2 + yl
    own = ((yh * NZ + z) * NC + core) * 2 + yl
    pair = ((yh * NZ + z) * NC + 1 - core) * 2 + yl
    scalars = jnp.stack(
        [core, y, audio_len[0], video_len[0], own * VT, pair * VT, z, own, *audio_pos]
    ).astype(jnp.int32)
    first = core == 0

    audio_cos, audio_sin = turn_tables(audio_pos)

    frequency = np.tile(ROPE_BASE ** (-np.arange(HD // 2) / (HD // 2)), 2).astype(np.float32)
    whole = pl.BlockSpec((AR, NC * CW), lambda g, sc: (0, 0))
    wide = pl.BlockSpec((AR, 4 * CW), lambda g, sc: (0, 0))
    keep, give = call(
        audio_kernel,
        scalars,
        (q_audio, k_audio, v_audio, d_audio, frequency[None]),
        [whole] * 4 + [pl.BlockSpec((1, HD), lambda g, sc: (0, 0))],
        [jax.ShapeDtypeStruct((AR, 4 * CW), bf16)] * 2,
        [wide] * 2,
        grid=(1,),
    )
    chip = jnp.concatenate([keep, shift(give, "core", NC, 1)], 0)

    def along_y(x):
        return [x] + [shift(x, Y, NY, NY - n) for n in range(1, NY)]

    def along_z(x):
        copies = jnp.broadcast_to(x[None], (NZ,) + x.shape).reshape(-1, x.shape[1])
        return lax.all_to_all(copies, "z", split_axis=0, concat_axis=0, tiled=True)

    kv, qd = chip[:, : 2 * CW], chip[:, 2 * CW :]
    home = jnp.concatenate(along_y(kv), 0)
    up, down = [home], [home]
    for _ in range(3):
        up.append(shift(up[-1], "z", NZ, NZ - 1))
        down.append(shift(down[-1], "z", NZ, 1))
    far = [shift(up[-1][: YR // 2], "z", NZ, NZ - 1), shift(down[-1][YR // 2 :], "z", NZ, 1)]
    kv_all = up + far + down[:0:-1]

    qd_z = along_z(qd)
    qd_all = along_y(qd_z)

    q_pair, k_pair, v_pair, d_pair = (
        shift(x, "core", NC, 1) for x in (q_video, k_video, v_video, d_video)
    )
    q_pair, k_pair, v_pair, d_pair, _ = lax.optimization_barrier(
        (q_pair, k_pair, v_pair, d_pair, qd_z)
    )
    cos, sin = turn_tables(jnp.stack([own * VT // VFRAME, pair * VT // VFRAME]))
    half = pl.BlockSpec((VT, GW), lambda g, sc: (0, sc[0] * GROUPS + g))
    table = pl.BlockSpec((2, HD), lambda g, sc: (0, 0))
    video_in = pl.BlockSpec((2 * VT, GW), lambda g, sc: (0, g))
    audio_in = pl.BlockSpec((ZR, 2 * GW), lambda g, sc: (0, g))
    video = pl.BlockSpec((2 * VT, GW), lambda g, sc: (0, g))
    audio = pl.BlockSpec((ZR, 2 * GW), lambda g, sc: (0, g))
    rows = pl.BlockSpec((2 * HEADS, AUDIO), lambda g, sc: (0, 0))
    mine = pl.BlockSpec((VT, GW), lambda g, sc: (0, g))
    video_shape = jax.ShapeDtypeStruct((2 * VT, CW), bf16)
    rows_shape = jax.ShapeDtypeStruct((2 * HEADS, AUDIO), f32)
    mine_shape = jax.ShapeDtypeStruct((VT, CW), bf16)
    audio_shape = jax.ShapeDtypeStruct((ZR, 2 * CW), bf16)
    one = 2 * 2 * VT * AUDIO * CW

    qr, kr, vr, dr = call(
        prepare_kernel,
        scalars,
        (q_video, q_pair, k_video, k_pair, v_video, v_pair, d_video, d_pair, cos, sin),
        [half] * 8 + [table] * 2,
        [video_shape] * 4,
        [video] * 4,
    )


    parts = call(
        video_to_audio_kernel,
        scalars,
        (qr, dr, *kv_all),
        [video_in] * 2 + [pl.BlockSpec((x.shape[0], 2 * GW), lambda g, sc: (0, g)) for x in kv_all],
        [audio_shape] * NY,
        [audio] * NY,
        flops=4 * one,
    )
    parts_y = [parts[0]] + [shift(parts[n], Y, NY, n) for n in range(1, NY)]

    kr, parts = lax.optimization_barrier((kr, parts))
    stats = call(
        statistics_kernel,
        scalars,
        (kr, vr, *qd_all),
        [video_in] * 2 + [audio_in] * NY,
        rows_shape,
        rows,
        flops=2 * one,
    )
    copies = jnp.broadcast_to(stats[None], (NZ,) + stats.shape)
    stats = lax.all_to_all(copies, "z", split_axis=0, concat_axis=0, tiled=True)
    stats = call(
        functools.partial(merge_kernel, count=NZ, turn=1),
        scalars,
        (stats,),
        [pl.BlockSpec(stats.shape, lambda g, sc: (0, 0, 0))],
        rows_shape,
        rows,
        grid=(1,),
        limit=16,
    )
    sums = call(
        sum_kernel,
        scalars,
        parts_y,
        [audio_in] * NY,
        audio_shape,
        audio,
        scratch=[pltpu.VMEM((2 * ZR, 2 * GW), f32)],
    )
    stats = call(
        functools.partial(merge_kernel, count=1, turn=-1),
        scalars,
        along_y(stats),
        [rows] * NY,
        rows_shape,
        rows,
        grid=(1,),
        limit=16,
    )
    dk0, dk1, dv0, dv1 = call(
        audio_to_video_kernel,
        scalars,
        (kr, vr, stats, cos, sin, *qd_all),
        [video_in] * 2 + [rows] + [table] * 2 + [audio_in] * NY,
        [mine_shape] * 4,
        [mine] * 4,
        flops=4 * one,
    )

    part = pl.BlockSpec((VT, CW), lambda g, sc: (0, 0))
    full = pl.BlockSpec((VT, NC * CW), lambda g, sc: (0, 0))
    dk_video, dv_video = call(
        join_kernel,
        scalars,
        (dk0, shift(dk1, "core", NC, 1), dv0, shift(dv1, "core", NC, 1)),
        [part] * 4,
        [jax.ShapeDtypeStruct((VT, NC * CW), bf16)] * 2,
        [full] * 2,
        grid=(1,),
    )
    sums = lax.all_to_all(sums, "z", split_axis=0, concat_axis=0, tiled=True)
    sums, _ = lax.optimization_barrier((sums, dk0))
    sums = jnp.sum(sums.reshape(NZ, CR, 2 * CW).astype(f32), 0)
    other = shift(sums[AR:], "core", NC, 1)
    sums = sums[:AR]
    sums = jnp.stack([jnp.where(first, sums, other), jnp.where(first, other, sums)], 1)
    sums = sums.reshape(AR, NC, GROUPS, 2, GW)
    dk_sum = sums[:, :, :, 0].reshape(AR, NC * CW)
    dk_audio = rotate_rows(dk_sum, audio_cos, -audio_sin).astype(bf16)
    dv_audio = sums[:, :, :, 1].reshape(AR, NC * CW).astype(bf16)
    return dk_video, dv_video, dk_audio, dv_audio


def solution(mesh):
    fine = Mesh(mesh.devices.reshape(mesh.shape["dp"], 2, NZ, NC, 2), ALL)
    rows = P(ALL, None)
    return jax.shard_map(
        local,
        mesh=fine,
        in_specs=(rows,) * 8 + (P(ALL), P("dp"), P("dp")),
        out_specs=(rows,) * 4,
        check_vma=False,
    )
```

```python
import functools
import math

import jax
import jax.numpy as jnp
import numpy as np
from jax import lax
from jax.experimental import pallas as pl
from jax.experimental.pallas import tpu as pltpu
from jax.sharding import Mesh
from jax.sharding import PartitionSpec as P

HD = 128
VFRAME = 512
ROPE_BASE = 10000.0
NEG = -1e30
SCALE = HD ** (-0.5)
LOG2E = math.log2(math.e)

NY, NZ, NC = 4, 8, 2
HEADS = 12
GROUPS = 2
HPG = HEADS // GROUPS
GW = HPG * HD
CW = HEADS * HD
VT = 128
AR = 4
CR = NC * AR
ZR = NZ * CR
YR = NY * CR
AUDIO = NY * ZR

ALL = ("dp", "yh", "z", "core", "yl")
Y = ("yh", "yl")
f32 = jnp.float32
bf16 = jnp.bfloat16


def frequencies():
    half = HD // 2
    return ROPE_BASE ** (-(jnp.arange(half, dtype=f32) / half))


def turn_tables(where_at):
    angle = where_at.astype(f32)[:, None] * frequencies()[None, :]
    cosine, sine = jnp.cos(angle), jnp.sin(angle)
    return jnp.concatenate([cosine, cosine], 1), jnp.concatenate([-sine, sine], 1)


def shift(x, axis, size, step):
    return lax.ppermute(x, axis, [(i, (i + step) % size) for i in range(size)])


def nt(a, b):
    return lax.dot_general(a, b, (((1,), (1,)), ((), ())), preferred_element_type=f32)


def nn(a, b):
    return lax.dot_general(a, b, (((1,), (0,)), ((), ())), preferred_element_type=f32)


def ahead(first, second):
    later = first(0)
    for i in range(HPG):
        now = later
        if i + 1 < HPG:
            later = first(i + 1)
        second(i, *now)


def head(i):
    return slice(i * HD, (i + 1) * HD)


def prepare_kernel(sc, q0, q1, k0, k1, v0, v1, d0, d1, cos, sin, qr, kr, vr, dr):
    limit = sc[3]
    for block, (q, k, v, d) in enumerate(((q0, k0, v0, d0), (q1, k1, v1, d1))):
        rows = slice(block * VT, (block + 1) * VT)
        cosine, sine = cos[block : block + 1, :], sin[block : block + 1, :]
        for i in range(HPG):
            for src, dst in ((q, qr), (k, kr)):
                x = src[:, head(i)].astype(f32)
                dst[rows, head(i)] = (
                    x * cosine + pltpu.roll(x, HD // 2, 1) * sine
                ).astype(bf16)
        vr[rows, :] = v[...]
        token = sc[4 + block] + lax.broadcasted_iota(jnp.int32, (VT, GW), 0)
        dr[rows, :] = jnp.where(token < limit, d[...].astype(f32), 0.0).astype(bf16)


def video_to_audio_kernel(sc, q, d, *refs):
    blocks, outs = refs[:NY], refs[NY:]
    core, y, limit = sc[0], sc[1], sc[2]
    row = lax.broadcasted_iota(jnp.int32, (AUDIO, HD), 0)
    yy = (row // ZR + y) % NY
    zz = (row // CR) % NZ
    r = row % CR
    cc = jnp.where(r < AR, core, 1 - core)
    own = ((yy // 2 * NZ + zz) * NC + cc) * 2 + yy % 2
    bias = jnp.where(own * AR + r % AR < limit, 0.0, NEG)
    bias = jnp.concatenate([bias, bias], 1)

    def scores(i):
        key = jnp.concatenate([a[:, head(i)] for a in blocks], 0)
        value = jnp.concatenate([a[:, head(HPG + i)] for a in blocks], 0)
        return nt(key, q[:, head(i)]), nt(value, d[:, head(i)])

    def gradients(i, s, dp):
        query, grad = q[:, head(i)], d[:, head(i)]
        s = s * (SCALE * LOG2E) + bias
        e = jnp.exp2(s - jnp.max(s, axis=0, keepdims=True))
        p = e * (1.0 / jnp.sum(e, axis=0, keepdims=True))
        pb = p.astype(bf16)
        delta = jnp.sum(p * dp, axis=0, keepdims=True)
        ds = (p * (dp - delta)).astype(bf16)
        dk = (nn(ds, query) * SCALE).astype(bf16)
        dv = nn(pb, grad).astype(bf16)
        for n, o in enumerate(outs):
            o[:, head(i)] = dk[n * ZR : (n + 1) * ZR]
            o[:, head(HPG + i)] = dv[n * ZR : (n + 1) * ZR]

    ahead(scores, gradients)


def sum_kernel(sc, p0, p1, p2, p3, out):
    out[...] = sum(p[...].astype(f32) for p in (p0, p1, p2, p3)).astype(bf16)


def pack_kernel(sc, keep, got, qd, copies):
    both = jnp.concatenate([keep[...].astype(f32), got[...].astype(f32)], 0)
    qd[...] = both[:, : 2 * CW].astype(bf16)
    kv = both[:, 2 * CW :]
    kv = jnp.concatenate([kv, kv], 0).astype(bf16)
    for n in range(NZ // 2):
        copies[n * 2 * CR : (n + 1) * 2 * CR, :] = kv


def audio_turn(sc, freq):
    row = lax.broadcasted_iota(jnp.int32, (AR, HD), 0)
    lane = lax.broadcasted_iota(jnp.int32, (AR, HD), 1)
    pos = functools.reduce(lambda a, n: jnp.where(row == n, sc[8 + n], a), range(1, AR), sc[8])
    angle = pos.astype(f32) * freq[...]
    cosine = jnp.cos(angle)
    sine = jnp.where(lane < HD // 2, -jnp.sin(angle), jnp.sin(angle))
    return cosine, sine


def audio_kernel(sc, q, k, v, d, freq, keep, give):
    core, own = sc[0], sc[7]
    cosine, sine = audio_turn(sc, freq)
    row = lax.broadcasted_iota(jnp.int32, (AR, HD), 0)
    ours = own * AR + row < sc[2]

    def turn(x):
        x = x.astype(f32)
        swapped = jnp.concatenate([x[:, HD // 2 :], x[:, : HD // 2]], 1)
        return x * cosine + swapped * sine

    def pair(ref, n, change):
        return [change(ref[:, head(c * HEADS + n)]) for c in range(NC)]

    same = lambda x: x.astype(f32)
    clear = lambda x: jnp.where(ours, x.astype(f32), 0.0)
    for n in range(HEADS):
        base = n // HPG * 2 * GW + n % HPG * HD
        for at, ref, change in ((base, q, turn), (base + GW, d, clear), (2 * CW + base, k, turn), (2 * CW + base + GW, v, same)):
            a, b = pair(ref, n, change)
            lanes = slice(at, at + HD)
            keep[:, lanes] = jnp.where(core == 0, a, b).astype(bf16)
            give[:, lanes] = jnp.where(core == 0, b, a).astype(bf16)


def video_token(sc, row):
    return jnp.where(row < VT, sc[4] + row, sc[5] + row - VT)


def statistics_kernel(sc, k, v, qd, copies, out):
    g = pl.program_id(0)
    row = lax.broadcasted_iota(jnp.int32, (2 * VT, HD), 0)
    bias = jnp.where(video_token(sc, row) < sc[3], 0.0, NEG)
    bias = jnp.concatenate([bias, bias], 1)
    some = jnp.minimum(sc[4], sc[5]) < sc[3]

    def scores(i):
        return nt(k[:, head(i)], qd[:, head(i)]), nt(v[:, head(i)], qd[:, head(HPG + i)])

    def sums(i, s, dp):
        s = s * (SCALE * LOG2E) + bias
        m = jnp.max(s, axis=0, keepdims=True)
        e = jnp.exp2(s - m)
        c = jnp.sum(e, axis=0, keepdims=True)
        t = jnp.sum(e * dp, axis=0, keepdims=True)
        out[pl.ds(g * HPG + i, 1), :] = jnp.where(some, m + jnp.log2(c), NEG)
        out[pl.ds(HEADS + g * HPG + i, 1), :] = jnp.where(some, t / c, 0.0)

    ahead(scores, sums)

    @pl.when(g == GROUPS - 1)
    def _():
        for n in range(NZ):
            copies[n] = out[...]


def merge(lses, deltas):
    top = functools.reduce(jnp.maximum, lses)
    weights = [jnp.exp2(x - top) for x in lses]
    total = sum(weights)
    delta = sum(w * x for w, x in zip(weights, deltas)) / total
    return top + jnp.log2(total), delta


def merge_kernel(sc, *refs, count, turn):
    *parts, out = refs
    if count > 1:
        (part,) = parts
        parts = [part.at[n] for n in range(count)]
    lse, delta = merge([p[:HEADS] for p in parts], [p[HEADS:] for p in parts])
    both = jnp.concatenate([lse, delta], 0)
    place = lax.broadcasted_iota(jnp.int32, both.shape, 1) // CR % NY
    if turn > 0:
        a = pltpu.roll(both, sc[1] * CR, 1)
        b = pltpu.roll(both, AUDIO - YR + sc[1] * CR, 1)
        out[...] = jnp.where(place >= sc[1], a, b)
    else:
        a = pltpu.roll(both, lax.rem(AUDIO - sc[1] * CR, AUDIO), 1)
        b = pltpu.roll(both, YR - sc[1] * CR, 1)
        out[...] = jnp.where(place < NY - sc[1], a, b)


def audio_to_video_kernel(sc, k, v, stats, cos, sin, qd, dk0, dk1, dv0, dv1):
    g = pl.program_id(0)
    row = lax.broadcasted_iota(jnp.int32, (2 * VT, HD), 0)
    valid = video_token(sc, row) < sc[3]

    def scores(i):
        query, grad = qd[:, head(i)], qd[:, head(HPG + i)]
        return query, grad, nt(k[:, head(i)], query), nt(v[:, head(i)], grad)

    def gradients(i, query, grad, s, dp):
        lse = stats[pl.ds(g * HPG + i, 1), :]
        delta = stats[pl.ds(HEADS + g * HPG + i, 1), :]
        p = jnp.exp2(s * (SCALE * LOG2E) - lse)
        ds = (p * (dp - delta)).astype(bf16)
        dv = jnp.where(valid, nn(p.astype(bf16), grad), 0.0).astype(bf16)
        dk = jnp.where(valid, nn(ds, query) * SCALE, 0.0)
        for block, (dko, dvo) in enumerate(((dk0, dv0), (dk1, dv1))):
            rows = slice(block * VT, (block + 1) * VT)
            x = dk[rows]
            dko[:, head(i)] = (
                x * cos[block : block + 1, :]
                - pltpu.roll(x, HD // 2, 1) * sin[block : block + 1, :]
            ).astype(bf16)
            dvo[:, head(i)] = dv[rows]

    ahead(scores, gradients)


def finish_kernel(sc, total, other, freq, dk, dv):
    core = sc[0]
    cosine, sine = audio_turn(sc, freq)
    for c in range(NC):
        mine = core == c
        for n in range(HEADS):
            base = n // HPG * 2 * GW + n % HPG * HD
            lanes = head(c * HEADS + n)
            x, w = (
                jnp.where(mine, total[:AR, at : at + HD], other[:, at : at + HD])
                for at in (base, base + GW)
            )
            swapped = jnp.concatenate([x[:, HD // 2 :], x[:, : HD // 2]], 1)
            dk[:, lanes] = (x * cosine - swapped * sine).astype(bf16)
            dv[:, lanes] = w.astype(bf16)


def join_kernel(sc, k1, v1, k, v, dk, dv):
    dk[...] = k1[...]
    dv[...] = v1[...]


def call(kernel, scalars, args, specs, outs, out_specs, grid=(GROUPS,), limit=16, scratch=(), aliases={}):
    return pl.pallas_call(
        kernel,
        grid_spec=pltpu.PrefetchScalarGridSpec(
            num_scalar_prefetch=1, grid=grid, in_specs=specs, out_specs=out_specs, scratch_shapes=scratch
        ),
        out_shape=outs,
        input_output_aliases=aliases,
        compiler_params=pltpu.CompilerParams(vmem_limit_bytes=limit * 1024 * 1024),
        cost_estimate=pl.CostEstimate(flops=0, bytes_accessed=0, transcendentals=0),
    )(scalars, *args)


def local(q_video, k_video, v_video, d_video, q_audio, k_audio, v_audio, d_audio, audio_pos, video_len, audio_len):
    yh, z, core, yl = (lax.axis_index(a) for a in ("yh", "z", "core", "yl"))
    y = yh * 2 + yl
    own = ((yh * NZ + z) * NC + core) * 2 + yl
    pair = ((yh * NZ + z) * NC + 1 - core) * 2 + yl
    scalars = jnp.stack(
        [core, y, audio_len[0], video_len[0], own * VT, pair * VT, z, own, *audio_pos]
    ).astype(jnp.int32)

    frequency = np.tile(ROPE_BASE ** (-np.arange(HD // 2) / (HD // 2)), 2).astype(np.float32)
    whole = pl.BlockSpec((AR, NC * CW), lambda g, sc: (0, 0))
    wide = pl.BlockSpec((AR, 4 * CW), lambda g, sc: (0, 0))
    keep, give = call(
        audio_kernel,
        scalars,
        (q_audio, k_audio, v_audio, d_audio, frequency[None]),
        [whole] * 4 + [pl.BlockSpec((1, HD), lambda g, sc: (0, 0))],
        [jax.ShapeDtypeStruct((AR, 4 * CW), bf16)] * 2,
        [wide] * 2,
        grid=(1,),
        limit=56,
    )
    chip = pl.BlockSpec((CR, 2 * CW), lambda g, sc: (0, 0))
    along = pl.BlockSpec((ZR, 2 * CW), lambda g, sc: (0, 0))
    qd, copies = call(
        pack_kernel,
        scalars,
        (keep, shift(give, "core", NC, 1)),
        [wide] * 2,
        [jax.ShapeDtypeStruct((CR, 2 * CW), bf16), jax.ShapeDtypeStruct((ZR, 2 * CW), bf16)],
        [chip, along],
        grid=(1,),
        limit=16,
    )
    kv_z = lax.all_to_all(copies, "z", split_axis=0, concat_axis=0, tiled=True)

    def along_y(x):
        return [x] + [shift(x, Y, NY, NY - n) for n in range(1, NY)]

    q_pair, k_pair, v_pair, d_pair = (
        shift(x, "core", NC, 1) for x in (q_video, k_video, v_video, d_video)
    )
    cos, sin = turn_tables(jnp.stack([own * VT // VFRAME, pair * VT // VFRAME]))
    half = pl.BlockSpec((VT, GW), lambda g, sc: (0, sc[0] * GROUPS + g))
    table = pl.BlockSpec((2, HD), lambda g, sc: (0, 0))
    video_in = pl.BlockSpec((2 * VT, GW), lambda g, sc: (0, g))
    all_in = pl.BlockSpec((AUDIO, 2 * GW), lambda g, sc: (0, g))
    audio_in = pl.BlockSpec((ZR, 2 * GW), lambda g, sc: (0, g))
    video = pl.BlockSpec((2 * VT, GW), lambda g, sc: (0, g))
    audio = pl.BlockSpec((ZR, 2 * GW), lambda g, sc: (0, g))
    rows = pl.BlockSpec((2 * HEADS, AUDIO), lambda g, sc: (0, 0))
    mine = pl.BlockSpec((VT, GW), lambda g, sc: (0, g))
    video_shape = jax.ShapeDtypeStruct((2 * VT, CW), bf16)
    rows_shape = jax.ShapeDtypeStruct((2 * HEADS, AUDIO), f32)
    full_shape = jax.ShapeDtypeStruct((VT, NC * CW), bf16)
    mine_shape = jax.ShapeDtypeStruct((VT, CW), bf16)
    audio_shape = jax.ShapeDtypeStruct((ZR, 2 * CW), bf16)

    qr, kr, vr, dr = call(
        prepare_kernel,
        scalars,
        (q_video, q_pair, k_video, k_pair, v_video, v_pair, d_video, d_pair, cos, sin),
        [half] * 8 + [table] * 2,
        [video_shape] * 4,
        [video] * 4,
    )


    home = jnp.concatenate(along_y(qd), 0)
    copies = jnp.broadcast_to(home[None], (NZ,) + home.shape).reshape(AUDIO, 2 * CW)
    copies, kv_z = lax.optimization_barrier((copies, kv_z))
    qd_all = lax.all_to_all(copies, "z", split_axis=0, concat_axis=0, tiled=True)
    kv_all = along_y(kv_z)

    parts = call(
        video_to_audio_kernel,
        scalars,
        (qr, dr, *kv_all),
        [video_in] * 2 + [audio_in] * NY,
        [audio_shape] * NY,
        [audio] * NY,
    )
    parts_y = [parts[0]] + [shift(parts[n], Y, NY, n) for n in range(1, NY)]

    kr, parts = lax.optimization_barrier((kr, parts))
    every = pl.BlockSpec((NZ, 2 * HEADS, AUDIO), lambda g, sc: (0, 0, 0))
    copies = call(
        statistics_kernel,
        scalars,
        (kr, vr, qd_all),
        [video_in] * 2 + [all_in],
        jax.ShapeDtypeStruct((NZ, 2 * HEADS, AUDIO), f32),
        every,
        scratch=[pltpu.VMEM((2 * HEADS, AUDIO), f32)],
    )
    stats = lax.all_to_all(copies, "z", split_axis=0, concat_axis=0, tiled=True)
    stats = call(
        functools.partial(merge_kernel, count=NZ, turn=1),
        scalars,
        (stats,),
        [every],
        rows_shape,
        rows,
        grid=(1,),
        limit=16,
    )
    sums = call(
        sum_kernel,
        scalars,
        parts_y,
        [audio_in] * NY,
        audio_shape,
        audio,
    )
    stats = call(
        functools.partial(merge_kernel, count=1, turn=-1),
        scalars,
        along_y(stats),
        [rows] * NY,
        rows_shape,
        rows,
        grid=(1,),
        limit=16,
    )
    dk0, dk1, dv0, dv1 = call(
        audio_to_video_kernel,
        scalars,
        (kr, vr, stats, cos, sin, qd_all),
        [video_in] * 2 + [rows] + [table] * 2 + [all_in],
        [full_shape, mine_shape] * 2,
        [half, mine] * 2,
    )

    dk_there = dk1
    dk1, dv1 = shift(dk1, "core", NC, 1), shift(dv1, "core", NC, 1)
    sums = lax.all_to_all(sums, "z", split_axis=0, concat_axis=0, tiled=True)
    sums, _ = lax.optimization_barrier((sums, dk_there))
    sums = jnp.sum(sums.reshape(NZ, CR, 2 * CW).astype(f32), 0)
    few = pl.BlockSpec((AR, NC * CW), lambda g, sc: (0, 0))
    dk_audio, dv_audio = call(
        finish_kernel,
        scalars,
        (sums, shift(sums[AR:], "core", NC, 1), frequency[None]),
        [chip, few, pl.BlockSpec((1, HD), lambda g, sc: (0, 0))],
        [jax.ShapeDtypeStruct((AR, NC * CW), bf16)] * 2,
        [few] * 2,
        grid=(1,),
        limit=16,
    )
    dk1, dv1, dk_audio, dv_audio = lax.optimization_barrier((dk1, dv1, dk_audio, dv_audio))
    place = pl.BlockSpec(memory_space=pl.ANY)
    other = pl.BlockSpec((VT, GW), lambda g, sc: (0, (1 - sc[0]) * GROUPS + g))
    dk_video, dv_video = call(
        join_kernel,
        scalars,
        (dk1, dv1, dk0, dv0),
        [mine] * 2 + [place] * 2,
        [full_shape] * 2,
        [other] * 2,
        aliases={3: 0, 4: 1},
        limit=16,
    )
    return dk_video, dv_video, dk_audio, dv_audio


def solution(mesh):
    fine = Mesh(mesh.devices.reshape(mesh.shape["dp"], 2, NZ, NC, 2), ALL)
    rows = P(ALL, None)
    return jax.shard_map(
        local,
        mesh=fine,
        in_specs=(rows,) * 8 + (P(ALL), P("dp"), P("dp")),
        out_specs=(rows,) * 4,
        check_vma=False,
    )
```

```python
import functools
import math

import jax
import jax.numpy as jnp
import numpy as np
from jax import lax
from jax.experimental import pallas as pl
from jax.experimental.pallas import tpu as pltpu
from jax.sharding import Mesh
from jax.sharding import PartitionSpec as P

HD = 128
VFRAME = 512
ROPE_BASE = 10000.0
NEG = -1e30
SCALE = HD ** (-0.5)
LOG2E = math.log2(math.e)

NY, NZ, NC = 4, 8, 2
HEADS = 12
GROUPS = 2
HPG = HEADS // GROUPS
GW = HPG * HD
CW = HEADS * HD
VT = 128
AR = 4
CR = NC * AR
ZR = NZ * CR
YR = NY * CR
AUDIO = NY * ZR

ALL = ("dp", "yh", "z", "core", "yl")
Y = ("yh", "yl")
f32 = jnp.float32
bf16 = jnp.bfloat16


def frequencies():
    half = HD // 2
    return ROPE_BASE ** (-(jnp.arange(half, dtype=f32) / half))


def turn_tables(where_at):
    angle = where_at.astype(f32)[:, None] * frequencies()[None, :]
    cosine, sine = jnp.cos(angle), jnp.sin(angle)
    return jnp.concatenate([cosine, cosine], 1), jnp.concatenate([-sine, sine], 1)


def shift(x, axis, size, step):
    return lax.ppermute(x, axis, [(i, (i + step) % size) for i in range(size)])


def nt(a, b):
    return lax.dot_general(a, b, (((1,), (1,)), ((), ())), preferred_element_type=f32)


def nn(a, b):
    return lax.dot_general(a, b, (((1,), (0,)), ((), ())), preferred_element_type=f32)


def ahead(first, second):
    later = first(0)
    for i in range(HPG):
        now = later
        if i + 1 < HPG:
            later = first(i + 1)
        second(i, *now)


def head(i):
    return slice(i * HD, (i + 1) * HD)


def prepare_kernel(sc, q0, q1, k0, k1, v0, v1, d0, d1, cos, sin, qr, kr, vr, dr):
    limit = sc[3]
    for block, (q, k, v, d) in enumerate(((q0, k0, v0, d0), (q1, k1, v1, d1))):
        rows = slice(block * VT, (block + 1) * VT)
        cosine, sine = cos[block : block + 1, :], sin[block : block + 1, :]
        for i in range(HPG):
            for src, dst in ((q, qr), (k, kr)):
                x = src[:, head(i)].astype(f32)
                dst[rows, head(i)] = (
                    x * cosine + pltpu.roll(x, HD // 2, 1) * sine
                ).astype(bf16)
        vr[rows, :] = v[...]
        token = sc[4 + block] + lax.broadcasted_iota(jnp.int32, (VT, GW), 0)
        dr[rows, :] = jnp.where(token < limit, d[...].astype(f32), 0.0).astype(bf16)


def video_to_audio_kernel(sc, q, d, *refs):
    blocks, outs = refs[:NY], refs[NY:]
    core, y, limit = sc[0], sc[1], sc[2]
    row = lax.broadcasted_iota(jnp.int32, (AUDIO, HD), 0)
    yy = (row // ZR + y) % NY
    zz = (row // CR) % NZ
    r = row % CR
    cc = jnp.where(r < AR, core, 1 - core)
    own = ((yy // 2 * NZ + zz) * NC + cc) * 2 + yy % 2
    bias = jnp.where(own * AR + r % AR < limit, 0.0, NEG)
    bias = jnp.concatenate([bias, bias], 1)

    def scores(i):
        key = jnp.concatenate([a[:, head(i)] for a in blocks], 0)
        value = jnp.concatenate([a[:, head(HPG + i)] for a in blocks], 0)
        return nt(key, q[:, head(i)]), nt(value, d[:, head(i)])

    def gradients(i, s, dp):
        query, grad = q[:, head(i)], d[:, head(i)]
        s = s * (SCALE * LOG2E) + bias
        e = jnp.exp2(s - jnp.max(s, axis=0, keepdims=True))
        p = e * (1.0 / jnp.sum(e, axis=0, keepdims=True))
        pb = p.astype(bf16)
        delta = jnp.sum(p * dp, axis=0, keepdims=True)
        ds = (p * (dp - delta)).astype(bf16)
        dk = (nn(ds, query) * SCALE).astype(bf16)
        dv = nn(pb, grad).astype(bf16)
        for n, o in enumerate(outs):
            o[:, head(i)] = dk[n * ZR : (n + 1) * ZR]
            o[:, head(HPG + i)] = dv[n * ZR : (n + 1) * ZR]

    ahead(scores, gradients)


def sum_kernel(sc, p0, p1, p2, p3, out):
    out[...] = sum(p[...].astype(f32) for p in (p0, p1, p2, p3)).astype(bf16)


def pack_kernel(sc, keep, got, qd, copies):
    both = jnp.concatenate([keep[...].astype(f32), got[...].astype(f32)], 0)
    qd[...] = both[:, : 2 * CW].astype(bf16)
    kv = both[:, 2 * CW :]
    kv = jnp.concatenate([kv, kv], 0).astype(bf16)
    for n in range(NZ // 2):
        copies[n * 2 * CR : (n + 1) * 2 * CR, :] = kv


def audio_turn(sc, freq):
    row = lax.broadcasted_iota(jnp.int32, (AR, HD), 0)
    lane = lax.broadcasted_iota(jnp.int32, (AR, HD), 1)
    pos = functools.reduce(lambda a, n: jnp.where(row == n, sc[8 + n], a), range(1, AR), sc[8])
    angle = pos.astype(f32) * freq[...]
    cosine = jnp.cos(angle)
    sine = jnp.where(lane < HD // 2, -jnp.sin(angle), jnp.sin(angle))
    return cosine, sine


def audio_kernel(sc, q, k, v, d, freq, keep, give):
    core, own = sc[0], sc[7]
    cosine, sine = audio_turn(sc, freq)
    row = lax.broadcasted_iota(jnp.int32, (AR, HD), 0)
    ours = own * AR + row < sc[2]

    def turn(x):
        x = x.astype(f32)
        swapped = jnp.concatenate([x[:, HD // 2 :], x[:, : HD // 2]], 1)
        return x * cosine + swapped * sine

    def pair(ref, n, change):
        return [change(ref[:, head(c * HEADS + n)]) for c in range(NC)]

    same = lambda x: x.astype(f32)
    clear = lambda x: jnp.where(ours, x.astype(f32), 0.0)
    for n in range(HEADS):
        base = n // HPG * 2 * GW + n % HPG * HD
        for at, ref, change in ((base, q, turn), (base + GW, d, clear), (2 * CW + base, k, turn), (2 * CW + base + GW, v, same)):
            a, b = pair(ref, n, change)
            lanes = slice(at, at + HD)
            keep[:, lanes] = jnp.where(core == 0, a, b).astype(bf16)
            give[:, lanes] = jnp.where(core == 0, b, a).astype(bf16)


def video_token(sc, row):
    return jnp.where(row < VT, sc[4] + row, sc[5] + row - VT)


def statistics_kernel(sc, k, v, *refs):
    *blocks, copies, out = refs
    g = pl.program_id(0)
    row = lax.broadcasted_iota(jnp.int32, (2 * VT, HD), 0)
    bias = jnp.where(video_token(sc, row) < sc[3], 0.0, NEG)
    bias = jnp.concatenate([bias, bias], 1)
    some = jnp.minimum(sc[4], sc[5]) < sc[3]

    def scores(i):
        query = jnp.concatenate([a[:, head(i)] for a in blocks], 0)
        grad = jnp.concatenate([a[:, head(HPG + i)] for a in blocks], 0)
        return nt(k[:, head(i)], query), nt(v[:, head(i)], grad)

    def sums(i, s, dp):
        s = s * (SCALE * LOG2E) + bias
        m = jnp.max(s, axis=0, keepdims=True)
        e = jnp.exp2(s - m)
        c = jnp.sum(e, axis=0, keepdims=True)
        t = jnp.sum(e * dp, axis=0, keepdims=True)
        out[pl.ds(g * HPG + i, 1), :] = jnp.where(some, m + jnp.log2(c), NEG)
        out[pl.ds(HEADS + g * HPG + i, 1), :] = jnp.where(some, t / c, 0.0)

    ahead(scores, sums)

    @pl.when(g == GROUPS - 1)
    def _():
        stats = pltpu.roll(out[...], sc[6] * YR, 1)
        for n in range(NZ):
            copies[n] = stats


def merge(lses, deltas):
    top = functools.reduce(jnp.maximum, lses)
    weights = [jnp.exp2(x - top) for x in lses]
    total = sum(weights)
    delta = sum(w * x for w, x in zip(weights, deltas)) / total
    return top + jnp.log2(total), delta


def merge_kernel(sc, *refs, count, turn):
    *parts, out = refs
    if count > 1:
        (part,) = parts
        parts = [part.at[n] for n in range(count)]
    lse, delta = merge([p[:HEADS] for p in parts], [p[HEADS:] for p in parts])
    both = jnp.concatenate([lse, delta], 0)
    place = lax.broadcasted_iota(jnp.int32, both.shape, 1) // CR % NY
    if turn > 0:
        a = pltpu.roll(both, sc[1] * CR, 1)
        b = pltpu.roll(both, AUDIO - YR + sc[1] * CR, 1)
        out[...] = jnp.where(place >= sc[1], a, b)
    else:
        a = pltpu.roll(both, lax.rem(AUDIO - sc[1] * CR, AUDIO), 1)
        b = pltpu.roll(both, YR - sc[1] * CR, 1)
        both = jnp.where(place < NY - sc[1], a, b)
        out[...] = pltpu.roll(both, lax.rem(AUDIO - sc[6] * YR, AUDIO), 1)


def audio_to_video_kernel(sc, k, v, stats, cos, sin, *refs):
    *blocks, dk0, dk1, dv0, dv1 = refs
    g = pl.program_id(0)
    row = lax.broadcasted_iota(jnp.int32, (2 * VT, HD), 0)
    valid = video_token(sc, row) < sc[3]

    def scores(i):
        query = jnp.concatenate([a[:, head(i)] for a in blocks], 0)
        grad = jnp.concatenate([a[:, head(HPG + i)] for a in blocks], 0)
        return query, grad, nt(k[:, head(i)], query), nt(v[:, head(i)], grad)

    def gradients(i, query, grad, s, dp):
        lse = stats[pl.ds(g * HPG + i, 1), :]
        delta = stats[pl.ds(HEADS + g * HPG + i, 1), :]
        p = jnp.exp2(s * (SCALE * LOG2E) - lse)
        ds = (p * (dp - delta)).astype(bf16)
        dv = jnp.where(valid, nn(p.astype(bf16), grad), 0.0).astype(bf16)
        dk = jnp.where(valid, nn(ds, query) * SCALE, 0.0)
        for block, (dko, dvo) in enumerate(((dk0, dv0), (dk1, dv1))):
            rows = slice(block * VT, (block + 1) * VT)
            x = dk[rows]
            dko[:, head(i)] = (
                x * cos[block : block + 1, :]
                - pltpu.roll(x, HD // 2, 1) * sin[block : block + 1, :]
            ).astype(bf16)
            dvo[:, head(i)] = dv[rows]

    ahead(scores, gradients)


def finish_kernel(sc, total, other, freq, dk, dv):
    core = sc[0]
    cosine, sine = audio_turn(sc, freq)
    for c in range(NC):
        mine = core == c
        for n in range(HEADS):
            base = n // HPG * 2 * GW + n % HPG * HD
            lanes = head(c * HEADS + n)
            x, w = (
                jnp.where(mine, total[:AR, at : at + HD], other[:, at : at + HD])
                for at in (base, base + GW)
            )
            swapped = jnp.concatenate([x[:, HD // 2 :], x[:, : HD // 2]], 1)
            dk[:, lanes] = (x * cosine - swapped * sine).astype(bf16)
            dv[:, lanes] = w.astype(bf16)


def join_kernel(sc, k1, v1, k, v, dk, dv):
    dk[...] = k1[...]
    dv[...] = v1[...]


def call(kernel, scalars, args, specs, outs, out_specs, grid=(GROUPS,), limit=16, scratch=(), aliases={}):
    return pl.pallas_call(
        kernel,
        grid_spec=pltpu.PrefetchScalarGridSpec(
            num_scalar_prefetch=1, grid=grid, in_specs=specs, out_specs=out_specs, scratch_shapes=scratch
        ),
        out_shape=outs,
        input_output_aliases=aliases,
        compiler_params=pltpu.CompilerParams(vmem_limit_bytes=limit * 1024 * 1024),
        cost_estimate=pl.CostEstimate(flops=0, bytes_accessed=0, transcendentals=0),
    )(scalars, *args)


def local(q_video, k_video, v_video, d_video, q_audio, k_audio, v_audio, d_audio, audio_pos, video_len, audio_len):
    yh, z, core, yl = (lax.axis_index(a) for a in ("yh", "z", "core", "yl"))
    y = yh * 2 + yl
    own = ((yh * NZ + z) * NC + core) * 2 + yl
    pair = ((yh * NZ + z) * NC + 1 - core) * 2 + yl
    scalars = jnp.stack(
        [core, y, audio_len[0], video_len[0], own * VT, pair * VT, z, own, *audio_pos]
    ).astype(jnp.int32)

    frequency = np.tile(ROPE_BASE ** (-np.arange(HD // 2) / (HD // 2)), 2).astype(np.float32)
    whole = pl.BlockSpec((AR, NC * CW), lambda g, sc: (0, 0))
    wide = pl.BlockSpec((AR, 4 * CW), lambda g, sc: (0, 0))
    keep, give = call(
        audio_kernel,
        scalars,
        (q_audio, k_audio, v_audio, d_audio, frequency[None]),
        [whole] * 4 + [pl.BlockSpec((1, HD), lambda g, sc: (0, 0))],
        [jax.ShapeDtypeStruct((AR, 4 * CW), bf16)] * 2,
        [wide] * 2,
        grid=(1,),
        limit=56,
    )
    chip = pl.BlockSpec((CR, 2 * CW), lambda g, sc: (0, 0))
    along = pl.BlockSpec((ZR, 2 * CW), lambda g, sc: (0, 0))
    qd, copies = call(
        pack_kernel,
        scalars,
        (keep, shift(give, "core", NC, 1)),
        [wide] * 2,
        [jax.ShapeDtypeStruct((CR, 2 * CW), bf16), jax.ShapeDtypeStruct((ZR, 2 * CW), bf16)],
        [chip, along],
        grid=(1,),
        limit=16,
    )
    kv_z = lax.all_to_all(copies, "z", split_axis=0, concat_axis=0, tiled=True)

    def along_y(x):
        return [x] + [shift(x, Y, NY, NY - n) for n in range(1, NY)]

    q_pair, k_pair, v_pair, d_pair = (
        shift(x, "core", NC, 1) for x in (q_video, k_video, v_video, d_video)
    )
    cos, sin = turn_tables(jnp.stack([own * VT // VFRAME, pair * VT // VFRAME]))
    half = pl.BlockSpec((VT, GW), lambda g, sc: (0, sc[0] * GROUPS + g))
    table = pl.BlockSpec((2, HD), lambda g, sc: (0, 0))
    video_in = pl.BlockSpec((2 * VT, GW), lambda g, sc: (0, g))
    audio_in = pl.BlockSpec((ZR, 2 * GW), lambda g, sc: (0, g))
    video = pl.BlockSpec((2 * VT, GW), lambda g, sc: (0, g))
    audio = pl.BlockSpec((ZR, 2 * GW), lambda g, sc: (0, g))
    rows = pl.BlockSpec((2 * HEADS, AUDIO), lambda g, sc: (0, 0))
    mine = pl.BlockSpec((VT, GW), lambda g, sc: (0, g))
    video_shape = jax.ShapeDtypeStruct((2 * VT, CW), bf16)
    rows_shape = jax.ShapeDtypeStruct((2 * HEADS, AUDIO), f32)
    full_shape = jax.ShapeDtypeStruct((VT, NC * CW), bf16)
    mine_shape = jax.ShapeDtypeStruct((VT, CW), bf16)
    audio_shape = jax.ShapeDtypeStruct((ZR, 2 * CW), bf16)

    qr, kr, vr, dr = call(
        prepare_kernel,
        scalars,
        (q_video, q_pair, k_video, k_pair, v_video, v_pair, d_video, d_pair, cos, sin),
        [half] * 8 + [table] * 2,
        [video_shape] * 4,
        [video] * 4,
        limit=56,
    )


    qd, qr, kr, vr, dr = lax.optimization_barrier((qd, qr, kr, vr, dr))
    home = jnp.concatenate(along_y(qd), 0)
    home, kv_z = lax.optimization_barrier((home, kv_z))
    kv_all = along_y(kv_z)
    up, down = [home], [home]
    for _ in range(3):
        up.append(shift(up[-1], "z", NZ, NZ - 1))
        down.append(shift(down[-1], "z", NZ, 1))
    up[3], down[3], *kv_all = lax.optimization_barrier((up[3], down[3], *kv_all))
    far = [shift(up[-1][: YR // 2], "z", NZ, NZ - 1), shift(down[-1][YR // 2 :], "z", NZ, 1)]
    qd_all = up + far + down[:0:-1]
    ring_in = [pl.BlockSpec((x.shape[0], 2 * GW), lambda g, sc: (0, g)) for x in qd_all]

    parts = call(
        video_to_audio_kernel,
        scalars,
        (qr, dr, *kv_all),
        [video_in] * 2 + [audio_in] * NY,
        [audio_shape] * NY,
        [audio] * NY,
    )
    parts_y = [parts[0]] + [shift(parts[n], Y, NY, n) for n in range(1, NY)]

    kr, parts = lax.optimization_barrier((kr, parts))
    every = pl.BlockSpec((NZ, 2 * HEADS, AUDIO), lambda g, sc: (0, 0, 0))
    copies = call(
        statistics_kernel,
        scalars,
        (kr, vr, *qd_all),
        [video_in] * 2 + ring_in,
        jax.ShapeDtypeStruct((NZ, 2 * HEADS, AUDIO), f32),
        every,
        scratch=[pltpu.VMEM((2 * HEADS, AUDIO), f32)],
    )
    stats = lax.all_to_all(copies, "z", split_axis=0, concat_axis=0, tiled=True)
    stats = call(
        functools.partial(merge_kernel, count=NZ, turn=1),
        scalars,
        (stats,),
        [every],
        rows_shape,
        rows,
        grid=(1,),
        limit=16,
    )
    sums = call(
        sum_kernel,
        scalars,
        parts_y,
        [audio_in] * NY,
        audio_shape,
        audio,
    )
    stats = call(
        functools.partial(merge_kernel, count=1, turn=-1),
        scalars,
        along_y(stats),
        [rows] * NY,
        rows_shape,
        rows,
        grid=(1,),
        limit=16,
    )
    dk0, dk1, dv0, dv1 = call(
        audio_to_video_kernel,
        scalars,
        (kr, vr, stats, cos, sin, *qd_all),
        [video_in] * 2 + [rows] + [table] * 2 + ring_in,
        [full_shape, mine_shape] * 2,
        [half, mine] * 2,
    )

    dk_there = dk1
    dk1, dv1 = shift(dk1, "core", NC, 1), shift(dv1, "core", NC, 1)
    sums = lax.all_to_all(sums, "z", split_axis=0, concat_axis=0, tiled=True)
    sums, _ = lax.optimization_barrier((sums, dk_there))
    sums = jnp.sum(sums.reshape(NZ, CR, 2 * CW).astype(f32), 0)
    few = pl.BlockSpec((AR, NC * CW), lambda g, sc: (0, 0))
    dk_audio, dv_audio = call(
        finish_kernel,
        scalars,
        (sums, shift(sums[AR:], "core", NC, 1), frequency[None]),
        [chip, few, pl.BlockSpec((1, HD), lambda g, sc: (0, 0))],
        [jax.ShapeDtypeStruct((AR, NC * CW), bf16)] * 2,
        [few] * 2,
        grid=(1,),
        limit=16,
    )
    place = pl.BlockSpec(memory_space=pl.ANY)
    other = pl.BlockSpec((VT, GW), lambda g, sc: (0, (1 - sc[0]) * GROUPS + g))
    dk_video, dv_video = call(
        join_kernel,
        scalars,
        (dk1, dv1, dk0, dv0),
        [mine] * 2 + [place] * 2,
        [full_shape] * 2,
        [other] * 2,
        aliases={3: 0, 4: 1},
        limit=16,
    )
    return dk_video, dv_video, dk_audio, dv_audio


def solution(mesh):
    fine = Mesh(mesh.devices.reshape(mesh.shape["dp"], 2, NZ, NC, 2), ALL)
    rows = P(ALL, None)
    return jax.shard_map(
        local,
        mesh=fine,
        in_specs=(rows,) * 8 + (P(ALL), P("dp"), P("dp")),
        out_specs=(rows,) * 4,
        check_vma=False,
    )
```

```python
import functools
import math

import jax
import jax.numpy as jnp
import numpy as np
from jax import lax
from jax.experimental import pallas as pl
from jax.experimental.pallas import tpu as pltpu
from jax.sharding import Mesh
from jax.sharding import PartitionSpec as P

HD = 128
VFRAME = 512
ROPE_BASE = 10000.0
NEG = -1e30
SCALE = HD ** (-0.5)
LOG2E = math.log2(math.e)

NY, NZ, NC = 4, 8, 2
HEADS = 12
GROUPS = 2
HPG = HEADS // GROUPS
GW = HPG * HD
CW = HEADS * HD
VT = 128
AR = 4
CR = NC * AR
ZR = NZ * CR
YR = NY * CR
AUDIO = NY * ZR

ALL = ("dp", "yh", "z", "core", "yl")
Y = ("yh", "yl")
f32 = jnp.float32
bf16 = jnp.bfloat16


def frequencies():
    half = HD // 2
    return ROPE_BASE ** (-(jnp.arange(half, dtype=f32) / half))


def turn_tables(where_at):
    angle = where_at.astype(f32)[:, None] * frequencies()[None, :]
    cosine, sine = jnp.cos(angle), jnp.sin(angle)
    return jnp.concatenate([cosine, cosine], 1), jnp.concatenate([-sine, sine], 1)


def shift(x, axis, size, step):
    return lax.ppermute(x, axis, [(i, (i + step) % size) for i in range(size)])


def nt(a, b):
    return lax.dot_general(a, b, (((1,), (1,)), ((), ())), preferred_element_type=f32)


def nn(a, b):
    return lax.dot_general(a, b, (((1,), (0,)), ((), ())), preferred_element_type=f32)


def ahead(first, second):
    later = first(0)
    for i in range(HPG):
        now = later
        if i + 1 < HPG:
            later = first(i + 1)
        second(i, *now)


def head(i):
    return slice(i * HD, (i + 1) * HD)


def prepare_kernel(sc, q0, q1, k0, k1, v0, v1, d0, d1, cos, sin, qr, kr, vr, dr):
    limit = sc[3]
    for block, (q, k, v, d) in enumerate(((q0, k0, v0, d0), (q1, k1, v1, d1))):
        rows = slice(block * VT, (block + 1) * VT)
        cosine, sine = cos[block : block + 1, :], sin[block : block + 1, :]
        for i in range(HPG):
            for src, dst in ((q, qr), (k, kr)):
                x = src[:, head(i)].astype(f32)
                dst[rows, head(i)] = (
                    x * cosine + pltpu.roll(x, HD // 2, 1) * sine
                ).astype(bf16)
        vr[rows, :] = v[...]
        token = sc[4 + block] + lax.broadcasted_iota(jnp.int32, (VT, GW), 0)
        dr[rows, :] = jnp.where(token < limit, d[...].astype(f32), 0.0).astype(bf16)


def video_to_audio_kernel(sc, q_far, d_far, *refs):
    blocks, outs, (q_near, d_near, sems) = refs[:NY], refs[NY : 2 * NY], refs[2 * NY :]
    g = pl.program_id(0)

    def moves(n):
        lanes = slice(n * GW, (n + 1) * GW)
        return [
            pltpu.make_async_copy(far.at[:, lanes], near.at[n], sems.at[m, n])
            for m, (far, near) in enumerate(((q_far, q_near), (d_far, d_near)))
        ]

    @pl.when(g == 0)
    def _():
        for n in range(GROUPS):
            for move in moves(n):
                move.start()

    for n in range(GROUPS):

        @pl.when(g == n)
        def _():
            for move in moves(n):
                move.wait()

    q, d = q_near.at[g], d_near.at[g]
    core, y, limit = sc[0], sc[1], sc[2]
    row = lax.broadcasted_iota(jnp.int32, (AUDIO, HD), 0)
    yy = (row // ZR + y) % NY
    zz = (row // CR) % NZ
    r = row % CR
    cc = jnp.where(r < AR, core, 1 - core)
    own = ((yy // 2 * NZ + zz) * NC + cc) * 2 + yy % 2
    bias = jnp.where(own * AR + r % AR < limit, 0.0, NEG)
    bias = jnp.concatenate([bias, bias], 1)

    def scores(i):
        key = jnp.concatenate([a[:, head(i)] for a in blocks], 0)
        value = jnp.concatenate([a[:, head(HPG + i)] for a in blocks], 0)
        return nt(key, q[:, head(i)]), nt(value, d[:, head(i)])

    def gradients(i, s, dp):
        query, grad = q[:, head(i)], d[:, head(i)]
        s = s * (SCALE * LOG2E) + bias
        e = jnp.exp2(s - jnp.max(s, axis=0, keepdims=True))
        p = e * (1.0 / jnp.sum(e, axis=0, keepdims=True))
        pb = p.astype(bf16)
        delta = jnp.sum(p * dp, axis=0, keepdims=True)
        ds = (p * (dp - delta)).astype(bf16)
        dk = (nn(ds, query) * SCALE).astype(bf16)
        dv = nn(pb, grad).astype(bf16)
        for n, o in enumerate(outs):
            o[:, head(i)] = dk[n * ZR : (n + 1) * ZR]
            o[:, head(HPG + i)] = dv[n * ZR : (n + 1) * ZR]

    ahead(scores, gradients)


def sum_kernel(sc, p0, p1, p2, p3, out):
    out[...] = sum(p[...].astype(f32) for p in (p0, p1, p2, p3)).astype(bf16)


def pack_kernel(sc, keep, got, qd, copies):
    both = jnp.concatenate([keep[...].astype(f32), got[...].astype(f32)], 0)
    qd[...] = both[:, : 2 * CW].astype(bf16)
    kv = both[:, 2 * CW :]
    kv = jnp.concatenate([kv, kv], 0).astype(bf16)
    for n in range(NZ // 2):
        copies[n * 2 * CR : (n + 1) * 2 * CR, :] = kv


def audio_turn(sc, freq):
    row = lax.broadcasted_iota(jnp.int32, (AR, HD), 0)
    lane = lax.broadcasted_iota(jnp.int32, (AR, HD), 1)
    pos = functools.reduce(lambda a, n: jnp.where(row == n, sc[8 + n], a), range(1, AR), sc[8])
    angle = pos.astype(f32) * freq[...]
    cosine = jnp.cos(angle)
    sine = jnp.where(lane < HD // 2, -jnp.sin(angle), jnp.sin(angle))
    return cosine, sine


def audio_kernel(sc, q, k, v, d, freq, keep, give):
    core, own = sc[0], sc[7]
    cosine, sine = audio_turn(sc, freq)
    row = lax.broadcasted_iota(jnp.int32, (AR, HD), 0)
    ours = own * AR + row < sc[2]

    def turn(x):
        x = x.astype(f32)
        swapped = jnp.concatenate([x[:, HD // 2 :], x[:, : HD // 2]], 1)
        return x * cosine + swapped * sine

    def pair(ref, n, change):
        return [change(ref[:, head(c * HEADS + n)]) for c in range(NC)]

    same = lambda x: x.astype(f32)
    clear = lambda x: jnp.where(ours, x.astype(f32), 0.0)
    for n in range(HEADS):
        base = n // HPG * 2 * GW + n % HPG * HD
        for at, ref, change in ((base, q, turn), (base + GW, d, clear), (2 * CW + base, k, turn), (2 * CW + base + GW, v, same)):
            a, b = pair(ref, n, change)
            lanes = slice(at, at + HD)
            keep[:, lanes] = jnp.where(core == 0, a, b).astype(bf16)
            give[:, lanes] = jnp.where(core == 0, b, a).astype(bf16)


def video_token(sc, row):
    return jnp.where(row < VT, sc[4] + row, sc[5] + row - VT)


def statistics_kernel(sc, k, v, *refs):
    *blocks, copies, out = refs
    g = pl.program_id(0)
    row = lax.broadcasted_iota(jnp.int32, (2 * VT, HD), 0)
    bias = jnp.where(video_token(sc, row) < sc[3], 0.0, NEG)
    bias = jnp.concatenate([bias, bias], 1)
    some = jnp.minimum(sc[4], sc[5]) < sc[3]

    def scores(i):
        query = jnp.concatenate([a[:, head(i)] for a in blocks], 0)
        grad = jnp.concatenate([a[:, head(HPG + i)] for a in blocks], 0)
        return nt(k[:, head(i)], query), nt(v[:, head(i)], grad)

    def sums(i, s, dp):
        s = s * (SCALE * LOG2E) + bias
        m = jnp.max(s, axis=0, keepdims=True)
        e = jnp.exp2(s - m)
        c = jnp.sum(e, axis=0, keepdims=True)
        t = jnp.sum(e * dp, axis=0, keepdims=True)
        out[pl.ds(g * HPG + i, 1), :] = jnp.where(some, m + jnp.log2(c), NEG)
        out[pl.ds(HEADS + g * HPG + i, 1), :] = jnp.where(some, t / c, 0.0)

    ahead(scores, sums)

    @pl.when(g == GROUPS - 1)
    def _():
        stats = pltpu.roll(out[...], sc[6] * YR, 1)
        for n in range(NZ):
            copies[n] = stats


def merge(lses, deltas):
    top = functools.reduce(jnp.maximum, lses)
    weights = [jnp.exp2(x - top) for x in lses]
    total = sum(weights)
    delta = sum(w * x for w, x in zip(weights, deltas)) / total
    return top + jnp.log2(total), delta


def merge_kernel(sc, parts, out):
    lse, delta = merge([parts[n, :HEADS] for n in range(NZ)], [parts[n, HEADS:] for n in range(NZ)])
    both = jnp.concatenate([lse, delta], 0)
    place = lax.broadcasted_iota(jnp.int32, both.shape, 1) // CR % NY
    a = pltpu.roll(both, sc[1] * CR, 1)
    b = pltpu.roll(both, AUDIO - YR + sc[1] * CR, 1)
    out[...] = jnp.where(place >= sc[1], a, b)


def merge_back(sc, parts):
    lse, delta = merge([p[:HEADS] for p in parts], [p[HEADS:] for p in parts])
    both = jnp.concatenate([lse, delta], 0)
    place = lax.broadcasted_iota(jnp.int32, both.shape, 1) // CR % NY
    a = pltpu.roll(both, lax.rem(AUDIO - sc[1] * CR, AUDIO), 1)
    b = pltpu.roll(both, YR - sc[1] * CR, 1)
    both = jnp.where(place < NY - sc[1], a, b)
    return pltpu.roll(both, lax.rem(AUDIO - sc[6] * YR, AUDIO), 1)


def audio_to_video_kernel(sc, k, v, s0, s1, s2, s3, cos, sin, *refs):
    *blocks, dk0, dk1, dv0, dv1, stats = refs
    g = pl.program_id(0)

    @pl.when(g == 0)
    def _():
        stats[...] = merge_back(sc, (s0, s1, s2, s3))

    row = lax.broadcasted_iota(jnp.int32, (2 * VT, HD), 0)
    valid = video_token(sc, row) < sc[3]

    def scores(i):
        query = jnp.concatenate([a[:, head(i)] for a in blocks], 0)
        grad = jnp.concatenate([a[:, head(HPG + i)] for a in blocks], 0)
        return query, grad, nt(k[:, head(i)], query), nt(v[:, head(i)], grad)

    def gradients(i, query, grad, s, dp):
        lse = stats[pl.ds(g * HPG + i, 1), :]
        delta = stats[pl.ds(HEADS + g * HPG + i, 1), :]
        p = jnp.exp2(s * (SCALE * LOG2E) - lse)
        ds = (p * (dp - delta)).astype(bf16)
        dv = jnp.where(valid, nn(p.astype(bf16), grad), 0.0).astype(bf16)
        dk = jnp.where(valid, nn(ds, query) * SCALE, 0.0)
        for block, (dko, dvo) in enumerate(((dk0, dv0), (dk1, dv1))):
            rows = slice(block * VT, (block + 1) * VT)
            x = dk[rows]
            dko[:, head(i)] = (
                x * cos[block : block + 1, :]
                - pltpu.roll(x, HD // 2, 1) * sin[block : block + 1, :]
            ).astype(bf16)
            dvo[:, head(i)] = dv[rows]

    ahead(scores, gradients)


def finish_audio(sc, total, other, freq, dk, dv):
    core = sc[0]
    cosine, sine = audio_turn(sc, freq)
    for c in range(NC):
        mine = core == c
        for n in range(HEADS):
            base = n // HPG * 2 * GW + n % HPG * HD
            lanes = head(c * HEADS + n)
            x, w = (
                jnp.where(mine, total[:AR, at : at + HD], other[:, at : at + HD])
                for at in (base, base + GW)
            )
            swapped = jnp.concatenate([x[:, HD // 2 :], x[:, : HD // 2]], 1)
            dk[:, lanes] = (x * cosine - swapped * sine).astype(bf16)
            dv[:, lanes] = w.astype(bf16)


def last_kernel(sc, k1, v1, k, v, total, other, freq, dk, dv, dk_audio, dv_audio):
    dk[...] = k1[...]
    dv[...] = v1[...]

    @pl.when(pl.program_id(0) == 0)
    def _():
        finish_audio(sc, total, other, freq, dk_audio, dv_audio)


def call(kernel, scalars, args, specs, outs, out_specs, grid=(GROUPS,), limit=16, scratch=(), aliases={}):
    return pl.pallas_call(
        kernel,
        grid_spec=pltpu.PrefetchScalarGridSpec(
            num_scalar_prefetch=1, grid=grid, in_specs=specs, out_specs=out_specs, scratch_shapes=scratch
        ),
        out_shape=outs,
        input_output_aliases=aliases,
        compiler_params=pltpu.CompilerParams(vmem_limit_bytes=limit * 1024 * 1024),
        cost_estimate=pl.CostEstimate(flops=0, bytes_accessed=0, transcendentals=0),
    )(scalars, *args)


def local(q_video, k_video, v_video, d_video, q_audio, k_audio, v_audio, d_audio, audio_pos, video_len, audio_len):
    yh, z, core, yl = (lax.axis_index(a) for a in ("yh", "z", "core", "yl"))
    y = yh * 2 + yl
    own = ((yh * NZ + z) * NC + core) * 2 + yl
    pair = ((yh * NZ + z) * NC + 1 - core) * 2 + yl
    scalars = jnp.stack(
        [core, y, audio_len[0], video_len[0], own * VT, pair * VT, z, own, *audio_pos]
    ).astype(jnp.int32)

    frequency = np.tile(ROPE_BASE ** (-np.arange(HD // 2) / (HD // 2)), 2).astype(np.float32)
    whole = pl.BlockSpec((AR, NC * CW), lambda g, sc: (0, 0))
    wide = pl.BlockSpec((AR, 4 * CW), lambda g, sc: (0, 0))
    keep, give = call(
        audio_kernel,
        scalars,
        (q_audio, k_audio, v_audio, d_audio, frequency[None]),
        [whole] * 4 + [pl.BlockSpec((1, HD), lambda g, sc: (0, 0))],
        [jax.ShapeDtypeStruct((AR, 4 * CW), bf16)] * 2,
        [wide] * 2,
        grid=(1,),
        limit=56,
    )
    chip = pl.BlockSpec((CR, 2 * CW), lambda g, sc: (0, 0))
    along = pl.BlockSpec((ZR, 2 * CW), lambda g, sc: (0, 0))
    qd, copies = call(
        pack_kernel,
        scalars,
        (keep, shift(give, "core", NC, 1)),
        [wide] * 2,
        [jax.ShapeDtypeStruct((CR, 2 * CW), bf16), jax.ShapeDtypeStruct((ZR, 2 * CW), bf16)],
        [chip, along],
        grid=(1,),
        limit=16,
    )
    kv_z = lax.all_to_all(copies, "z", split_axis=0, concat_axis=0, tiled=True)

    def along_y(x):
        return [x] + [shift(x, Y, NY, NY - n) for n in range(1, NY)]

    q_pair, k_pair, v_pair, d_pair = (
        shift(x, "core", NC, 1) for x in (q_video, k_video, v_video, d_video)
    )
    cos, sin = turn_tables(jnp.stack([own * VT // VFRAME, pair * VT // VFRAME]))
    half = pl.BlockSpec((VT, GW), lambda g, sc: (0, sc[0] * GROUPS + g))
    table = pl.BlockSpec((2, HD), lambda g, sc: (0, 0))
    video_in = pl.BlockSpec((2 * VT, GW), lambda g, sc: (0, g))
    audio_in = pl.BlockSpec((ZR, 2 * GW), lambda g, sc: (0, g))
    video = pl.BlockSpec((2 * VT, GW), lambda g, sc: (0, g))
    audio = pl.BlockSpec((ZR, 2 * GW), lambda g, sc: (0, g))
    rows = pl.BlockSpec((2 * HEADS, AUDIO), lambda g, sc: (0, 0))
    mine = pl.BlockSpec((VT, GW), lambda g, sc: (0, g))
    video_shape = jax.ShapeDtypeStruct((2 * VT, CW), bf16)
    rows_shape = jax.ShapeDtypeStruct((2 * HEADS, AUDIO), f32)
    full_shape = jax.ShapeDtypeStruct((VT, NC * CW), bf16)
    mine_shape = jax.ShapeDtypeStruct((VT, CW), bf16)
    audio_shape = jax.ShapeDtypeStruct((ZR, 2 * CW), bf16)

    qr, kr, vr, dr = call(
        prepare_kernel,
        scalars,
        (q_video, q_pair, k_video, k_pair, v_video, v_pair, d_video, d_pair, cos, sin),
        [half] * 8 + [table] * 2,
        [video_shape] * 4,
        [video] * 4,
        limit=56,
    )


    qd, qr, kr, vr, dr = lax.optimization_barrier((qd, qr, kr, vr, dr))
    home = jnp.concatenate(along_y(qd), 0)
    home, kv_z = lax.optimization_barrier((home, kv_z))
    kv_all = along_y(kv_z)
    up, down = [home], [home]
    for _ in range(3):
        up.append(shift(up[-1], "z", NZ, NZ - 1))
        down.append(shift(down[-1], "z", NZ, 1))
    up[3], down[3], *kv_all = lax.optimization_barrier((up[3], down[3], *kv_all))
    far = [shift(up[-1][: YR // 2], "z", NZ, NZ - 1), shift(down[-1][YR // 2 :], "z", NZ, 1)]
    qd_all = up + far + down[:0:-1]
    ring_in = [pl.BlockSpec((x.shape[0], 2 * GW), lambda g, sc: (0, g)) for x in qd_all]

    parts = call(
        video_to_audio_kernel,
        scalars,
        (qr, dr, *kv_all),
        [pl.BlockSpec(memory_space=pltpu.HBM)] * 2 + [audio_in] * NY,
        [audio_shape] * NY,
        [audio] * NY,
        scratch=[pltpu.VMEM((GROUPS, 2 * VT, GW), bf16)] * 2
        + [pltpu.SemaphoreType.DMA((2, GROUPS))],
        limit=58,
    )
    parts_y = [parts[0]] + [shift(parts[n], Y, NY, n) for n in range(1, NY)]

    kr, parts = lax.optimization_barrier((kr, parts))
    every = pl.BlockSpec((NZ, 2 * HEADS, AUDIO), lambda g, sc: (0, 0, 0))
    copies = call(
        statistics_kernel,
        scalars,
        (kr, vr, *qd_all),
        [video_in] * 2 + ring_in,
        jax.ShapeDtypeStruct((NZ, 2 * HEADS, AUDIO), f32),
        every,
        scratch=[pltpu.VMEM((2 * HEADS, AUDIO), f32)],
    )
    stats = lax.all_to_all(copies, "z", split_axis=0, concat_axis=0, tiled=True)
    stats = call(
        merge_kernel,
        scalars,
        (stats,),
        [every],
        rows_shape,
        rows,
        grid=(1,),
        limit=16,
    )
    sums = call(
        sum_kernel,
        scalars,
        parts_y,
        [audio_in] * NY,
        audio_shape,
        audio,
    )
    dk0, dk1, dv0, dv1 = call(
        audio_to_video_kernel,
        scalars,
        (kr, vr, *along_y(stats), cos, sin, *qd_all),
        [video_in] * 2 + [rows] * NY + [table] * 2 + ring_in,
        [full_shape, mine_shape] * 2,
        [half, mine] * 2,
        scratch=[pltpu.VMEM((2 * HEADS, AUDIO), f32)],
    )

    dk_there = dk1
    dk1, dv1 = shift(dk1, "core", NC, 1), shift(dv1, "core", NC, 1)
    sums = lax.all_to_all(sums, "z", split_axis=0, concat_axis=0, tiled=True)
    sums, _ = lax.optimization_barrier((sums, dk_there))
    sums = jnp.sum(sums.reshape(NZ, CR, 2 * CW).astype(f32), 0)
    few = pl.BlockSpec((AR, NC * CW), lambda g, sc: (0, 0))
    place = pl.BlockSpec(memory_space=pl.ANY)
    other = pl.BlockSpec((VT, GW), lambda g, sc: (0, (1 - sc[0]) * GROUPS + g))
    dk_video, dv_video, dk_audio, dv_audio = call(
        last_kernel,
        scalars,
        (dk1, dv1, dk0, dv0, sums, shift(sums[AR:], "core", NC, 1), frequency[None]),
        [mine] * 2 + [place] * 2 + [chip, few, pl.BlockSpec((1, HD), lambda g, sc: (0, 0))],
        [full_shape] * 2 + [jax.ShapeDtypeStruct((AR, NC * CW), bf16)] * 2,
        [other] * 2 + [few] * 2,
        aliases={3: 0, 4: 1},
        limit=16,
    )
    return dk_video, dv_video, dk_audio, dv_audio


def solution(mesh):
    fine = Mesh(mesh.devices.reshape(mesh.shape["dp"], 2, NZ, NC, 2), ALL)
    rows = P(ALL, None)
    return jax.shard_map(
        local,
        mesh=fine,
        in_specs=(rows,) * 8 + (P(ALL), P("dp"), P("dp")),
        out_specs=(rows,) * 4,
        check_vma=False,
    )
```
